32 devices in a mesh: ctx: 16 (over z, y, core), head: 2 (over x).
Axes of the slice: x: 2, y: 2, z: 4, core: 2. Of those that a mesh axis runs over, the one named last changes fastest.
Arguments:
- messages: bfloat16 [65536, 1024], P('ctx', 'head'), may hold values from -6 to 6
- node_anchor: int32 [65536], P('ctx'), may hold values from 0 to 4095, as said below
- anchor_count: int32 [16], P('ctx'), may hold values from 48 to 192, as said below
- norm_gain: float32 [1024], replicated, may hold values from 0.5 to 1.5
- w_query: bfloat16 [1024, 1024], P(None, 'head'), may hold values from -16 to 16
- w_key: bfloat16 [1024, 1024], P(None, 'head'), may hold values from -0.3125 to 0.3125
- w_value: bfloat16 [1024, 1024], P(None, 'head'), may hold values from -0.1875 to 0.1875
- w_out: bfloat16 [1024, 1024], P(None, 'head'), may hold values from -0.25 to 0.25
Outputs:
- anchor_out: bfloat16 [4096, 1024], P('ctx', 'head')
The draws below stay inside these ranges and needn't reach their ends.
Inputs may be any that keep to these rules, and one draw needn't show every extreme that they name: node_anchor[n] names a live anchor (its slot within the partition is below that partition's anchor_count); its partition is the partition of node n or one of the two partitions beside it, counted cyclically; all 128 nodes of an aligned tile of 128 nodes have the same anchor partition; every partition has tiles pooled into each of its two neighbours. `anchor_count`: some partition has exactly 192 live anchors.
All inputs are finite; a program needn't handle non-finite values.
Results may differ from the reference program's by a relative error of at most 0.006.
The reference program's roundings to bfloat16 on the way (of `pooled`, `normed` and `attended`) count: a program that leaves them out, or rounds other values in their place, can miss the bound.
Values may be sent and summed in bfloat16 or wider, within the bound.
No kernel may reach another device: no remote copies, remote signals or barrier semaphores. Data moves between devices by JAX's collectives and lax.ppermute only.
A program may use at most 128 MiB of HBM per device.

```python
import math
import jax
import jax.numpy as jnp
from jax import lax

D = 1024
HEADS = 16
HD = 64
NODE_DEV = 4096
ANCH_DEV = 256
LIVE_MAX = 192
NODES = 65536
ANCH = 4096


def anchor_layout(key):
    count_key, top_key = jax.random.split(jax.random.fold_in(key, 7))
    partitions = ANCH // ANCH_DEV
    counts = jax.random.randint(count_key, (partitions,), LIVE_MAX // 4, LIVE_MAX + 1)
    fullest = jax.random.randint(top_key, (), 0, partitions)
    counts = jnp.where(jnp.arange(partitions) == fullest, LIVE_MAX, counts)
    return counts.astype(jnp.int32)


def draw_anchor_count(key, part):
    return anchor_layout(key)


def draw_node_anchor(key, part):
    counts = anchor_layout(key)
    partitions = NODES // NODE_DEV
    tiles = NODES // 128
    tiles_per = NODE_DEV // 128
    side_key, slot_key = jax.random.split(jax.random.fold_in(key, 11))
    sides = jax.random.randint(side_key, (tiles,), 0, 4)
    moves = jnp.where(sides == 0, -1, jnp.where(sides == 3, 1, 0))
    tile_index = jnp.arange(tiles, dtype=jnp.int32)
    position = tile_index % tiles_per
    moves = jnp.where(position == 0, -1, jnp.where(position == 1, 1, moves))
    tile_home = tile_index // tiles_per
    owners = (tile_home + moves + partitions) % partitions
    node_owner = jnp.repeat(owners, 128)
    limits = counts[node_owner]
    slots = jax.random.randint(slot_key, (NODES,), 0, limits)
    return (node_owner * ANCH_DEV + slots).astype(jnp.int32)


def draw_w_query(key, part):
    base_key = jax.random.fold_in(jax.random.fold_in(key, 3), 0)
    values = jnp.clip(jax.random.normal(base_key, (D, D), jnp.float32), -6.0, 6.0) * jnp.sqrt(3.0 / D)
    return jnp.clip(values, -16.0, 16.0).astype(jnp.bfloat16)


def strengthened(values, stream_key, source, target, parts, factor):
    owner, partner = [(jnp.arange(values.shape[axis_at]) // (values.shape[axis_at] // parts)).reshape([-1 if axis == axis_at else 1 for axis in range(values.ndim)]) for axis_at in (source, target)]
    chosen = jax.random.permutation(stream_key, parts)[partner]
    strong = (owner == chosen) | (owner == (partner + parts // 2) % parts)
    return jnp.where(strong, factor * values, values)


def block_scale(key, extent, cuts, low, high):
    loudness, own = 1.0, jax.random.fold_in(key, 6)
    for axis_at, shards_of in cuts:
        draws = jnp.exp(jax.random.uniform(jax.random.fold_in(own, axis_at), (shards_of,), jnp.float32, low / len(cuts), high / len(cuts)))
        loudness = loudness * jnp.repeat(draws, extent[axis_at] // shards_of).reshape([-1 if axis == axis_at else 1 for axis in range(len(extent))])
    return loudness


def noise(key, shape, spread, limit, cuts=(), kind=jnp.bfloat16):
    gain = block_scale(key, shape, cuts, -0.22, 0.18) if cuts else 1.0
    values = jax.random.normal(key, shape, jnp.float32) * spread * gain
    return jnp.minimum(jnp.maximum(values, -limit), limit).astype(kind)


def heavy_noise(own_key, dims, spread, reach, shards, heavy, kind=jnp.bfloat16):
    entries = spread * jax.random.normal(own_key, dims, jnp.float32)
    if shards:
        entries = entries * block_scale(own_key, dims, shards, -0.22, 0.18)
    return jnp.clip(strengthened(entries, jax.random.fold_in(own_key, 3), *heavy), -reach, reach).astype(kind)


def setup_inputs(seed: int = 0) -> dict:
    keys = jax.random.split(jax.random.key(seed), 9)
    return {
        "messages": noise(keys[0], (NODES, D), 1.0, 6.0, ((0, 16), (1, 2))),
        "node_anchor": draw_node_anchor(jax.random.fold_in(keys[8], 71), 0),
        "anchor_count": draw_anchor_count(jax.random.fold_in(keys[8], 71), 0),
        "norm_gain": jnp.clip(1.0 + 0.1 * jax.random.normal(keys[3], (D,), jnp.float32), 0.5, 1.5),
        "w_query": draw_w_query(jax.random.fold_in(keys[8], 71), 0),
        "w_key": noise(keys[5], (D, D), (D // 3) ** -0.5, 0.3125, ((1, 2),)),
        "w_value": noise(keys[6], (D, D), D ** -0.5, 0.1875, ((1, 2),)),
        "w_out": heavy_noise(keys[7], (D, D), D ** -0.5, 0.25, ((1, 2),), (0, 1, 2, 2.0)),
    }


EPS = 1e-06
NEG = -1e+30

def reference(messages, node_anchor, anchor_count, norm_gain, w_query, w_key, w_value, w_out):
    sums = jax.ops.segment_sum(messages.astype(jnp.float32), node_anchor, num_segments=ANCH)
    pooled = lax.optimization_barrier(sums.astype(jnp.bfloat16)).astype(jnp.float32)
    mean_square = lax.optimization_barrier(jnp.mean(pooled * pooled, axis=1, keepdims=True))
    normed = (pooled * lax.rsqrt(mean_square + EPS) * norm_gain).astype(jnp.bfloat16)
    queries = jnp.dot(normed, w_query, preferred_element_type=jnp.float32).astype(jnp.bfloat16)
    keys_all = jnp.dot(normed, w_key, preferred_element_type=jnp.float32).astype(jnp.bfloat16)
    values_all = jnp.dot(normed, w_value, preferred_element_type=jnp.float32).astype(jnp.bfloat16)
    slots = jnp.arange(ANCH, dtype=jnp.int32)
    alive = slots % ANCH_DEV < anchor_count[slots // ANCH_DEV]
    block_rows = math.gcd(ANCH, 512)
    scale = HD ** (-0.5)

    def one_head(index):
        head_q = lax.dynamic_slice_in_dim(queries, index * HD, HD, 1)
        head_k = lax.dynamic_slice_in_dim(keys_all, index * HD, HD, 1)
        head_v = lax.dynamic_slice_in_dim(values_all, index * HD, HD, 1)

        def one_block(query_block):
            scores = jnp.dot(query_block, head_k.T, preferred_element_type=jnp.float32) * scale
            scores = jnp.where(alive[None, :], scores, NEG)
            highest = lax.optimization_barrier(jnp.max(scores, axis=1, keepdims=True))
            weights = jnp.where(alive[None, :], jnp.exp(scores - highest), 0.0)
            totals = lax.optimization_barrier(jnp.sum(weights, axis=1, keepdims=True))
            mixed = jnp.dot(weights.astype(jnp.bfloat16), head_v, preferred_element_type=jnp.float32)
            return (mixed / totals).astype(jnp.bfloat16)
        blocks = head_q.reshape(ANCH // block_rows, block_rows, HD)
        return lax.map(one_block, blocks).reshape(ANCH, HD)
    attended = lax.map(one_head, jnp.arange(HEADS, dtype=jnp.int32))
    attended = attended.transpose(1, 0, 2).reshape(ANCH, D)
    branch = jnp.dot(attended, w_out, preferred_element_type=jnp.float32)
    return (normed.astype(jnp.float32) + branch).astype(jnp.bfloat16)
```

```python
import functools
import math

import jax
import jax.numpy as jnp
from jax import lax
from jax.experimental import pallas as pl
from jax.experimental.pallas import tpu as pltpu
from jax.sharding import PartitionSpec as P

HD = 64
ANCH_DEV = 256
LIVE_MAX = 192
HALF = LIVE_MAX // 2
PAD = 16
QROWS = 2 * LIVE_MAX + PAD
TILE = 128

EPS = 1e-06
NEG = -1e30
MARK = 2.0**100
MARKED = 2.0**90
RATE = HD**-0.5 * math.log2(math.e)

ALL = ("ctx", "head")
F32 = jnp.float32
BF16 = jnp.bfloat16


def params(mib=32):
    return pltpu.CompilerParams(vmem_limit_bytes=mib * 2**20)


def vmem(count):
    return [pl.BlockSpec(memory_space=pltpu.VMEM)] * count


def dot(a, b, contract=((1,), (0,))):
    return lax.dot_general(a, b, (contract, ((), ())), preferred_element_type=F32)


def row_of(slot):
    block = slot // 16
    return (block % 2) * HALF + (block // 2) * 16 + slot % 16


def pool_kernel(tiles, anchors_smem, anchors_ref, messages_ref, before_ref, own_ref, after_ref, sums):
    step = pl.program_id(0)
    partitions = lax.axis_size("ctx")
    center = lax.axis_index("ctx")

    @pl.when(step == 0)
    def _():
        sums[...] = jnp.zeros_like(sums)

    rows = lax.broadcasted_iota(jnp.int32, (LIVE_MAX, TILE), 0)
    for tile in range(tiles):
        index = step * tiles + tile
        owner = anchors_smem[index * TILE] // ANCH_DEV
        side = lax.rem(owner - center + 1 + partitions, partitions)
        slot = row_of(anchors_ref[pl.ds(index, 1), :] % ANCH_DEV)
        onehot = jnp.where(rows == slot, 1.0, 0.0).astype(BF16)
        part = dot(onehot, messages_ref[tile * TILE : (tile + 1) * TILE, :])
        sums[side] += part

    @pl.when(step == pl.num_programs(0) - 1)
    def _():
        before_ref[...] = sums[0]
        own_ref[...] = sums[1]
        after_ref[...] = sums[2]


def pool(messages, node_anchor):
    nodes, channels = messages.shape
    steps = 8
    tiles = nodes // TILE // steps
    shape = jax.ShapeDtypeStruct((LIVE_MAX, channels), F32)
    whole = pl.BlockSpec((LIVE_MAX, channels), lambda i, a: (0, 0))
    return pl.pallas_call(
        functools.partial(pool_kernel, tiles),
        grid_spec=pltpu.PrefetchScalarGridSpec(
            num_scalar_prefetch=1,
            grid=(steps,),
            in_specs=[
                pl.BlockSpec((nodes // TILE, TILE), lambda i, a: (0, 0)),
                pl.BlockSpec((tiles * TILE, channels), lambda i, a: (i, 0)),
            ],
            out_specs=[whole] * 3,
            scratch_shapes=[pltpu.VMEM((3, LIVE_MAX, channels), F32)],
        ),
        out_shape=[shape] * 3,
        compiler_params=params(),
        name="pool",
    )(node_anchor, node_anchor.reshape(nodes // TILE, TILE), messages)


def settle_kernel(count_ref, own_ref, before_ref, after_ref, keep_ref, send_ref):
    core = lax.rem(lax.axis_index("ctx"), 2)
    count = count_ref[0]

    def half(which):
        at = pl.ds(pl.multiple_of(which * HALF, 16), HALF)
        total = own_ref[at, :] + before_ref[at, :] + after_ref[at, :]
        row = lax.broadcasted_iota(jnp.int32, total.shape, 0)
        slot = (2 * (row // 16) + which) * 16 + row % 16
        return jnp.where(slot < count, total, MARK).astype(BF16)

    keep_ref[...] = half(core)
    send_ref[...] = half(1 - core)


def settle(count, own, before, after):
    channels = own.shape[1]
    shape = jax.ShapeDtypeStruct((HALF, channels), BF16)
    return pl.pallas_call(
        settle_kernel,
        in_specs=[pl.BlockSpec(memory_space=pltpu.SMEM)] + vmem(3),
        out_specs=vmem(2),
        out_shape=[shape] * 2,
        compiler_params=params(),
        name="settle",
    )(count, own, before, after)


def normalise(mine, other, gain_ref, x):
    channels = mine.shape[1]
    mine, other = mine.astype(F32), other.astype(F32)
    dead = mine[:, :1] > MARKED
    mine = jnp.where(dead, 0.0, mine)
    other = jnp.where(dead, 0.0, other)
    square = jnp.sum(mine * mine + other * other, axis=1, keepdims=True)
    inverse = lax.rsqrt(square * (1.0 / (2 * channels)) + EPS)
    mine = (mine * inverse * gain_ref[x]).astype(BF16)
    other = (other * inverse * gain_ref[1 - x]).astype(BF16)
    return mine, other, dead


def project(mine, other, w_ref, x):
    return (dot(mine, w_ref[x]) + dot(other, w_ref[1 - x])).astype(BF16)


def query_kernel(own_ref, first_ref, second_ref, gain_ref, wq_ref, swap_ref, normed_ref):
    core = lax.rem(lax.axis_index("ctx"), 2)
    x = lax.axis_index("head")
    other = jnp.where(core == 0, second_ref[:LIVE_MAX, :], first_ref[...])
    mine, other, unused = normalise(own_ref[...], other, gain_ref, x)
    swap_ref[:LIVE_MAX, :] = project(mine, other, wq_ref, x)
    swap_ref[LIVE_MAX:, :] = mine[HALF:]
    normed_ref[...] = mine[:HALF]


def make_queries(own, first, second, gain, wq):
    channels = own.shape[1]
    return pl.pallas_call(
        query_kernel,
        in_specs=vmem(5),
        out_specs=vmem(2),
        out_shape=[
            jax.ShapeDtypeStruct((LIVE_MAX + HALF, channels), BF16),
            jax.ShapeDtypeStruct((HALF, channels), BF16),
        ],
        compiler_params=params(),
        cost_estimate=pl.CostEstimate(flops=4 * 10**8, bytes_accessed=2 * 10**6, transcendentals=0),
        name="queries",
    )(own, first, second, gain, wq)


def attend_kernel(first_call, *refs):
    if first_call:
        qm, qr, own_ref, first_ref, second_ref, gain_ref, wk_ref, wv_ref, out_ref = refs
        state_ref = None
    else:
        qm, qr, own_ref, first_ref, second_ref, gain_ref, wk_ref, wv_ref, state_ref, out_ref = refs
    core = lax.rem(lax.axis_index("ctx"), 2)
    x = lax.axis_index("head")
    channels = own_ref.shape[1]
    heads = channels // HD
    one, two = first_ref[...], second_ref[:LIVE_MAX, :]
    mine = jnp.concatenate([own_ref[...], jnp.where(core == 0, one, two)], axis=0)
    other = jnp.concatenate([jnp.where(core == 0, two, one), second_ref[LIVE_MAX:, :]], axis=0)
    mine, other, dead = normalise(mine, other, gain_ref, x)
    keys = project(mine, other, wk_ref, x)
    values = project(mine, other, wv_ref, x)
    shut = jnp.where(dead, NEG, 0.0).astype(BF16)

    lane_k = lax.broadcasted_iota(jnp.int32, (keys.shape[0], 128), 1)
    lane_q = lax.broadcasted_iota(jnp.int32, (QROWS, 128), 1)
    lane_a = lax.broadcasted_iota(jnp.int32, (QROWS, 128), 1)
    tops = jnp.full((QROWS, 128), 0.0, F32) if first_call else state_ref[:, channels:]
    stats = tops
    for pair in range(heads // 2):
        at = slice(pair * 128, (pair + 1) * 128)
        query = jnp.concatenate(
            [qm[:HALF, at], qr[HALF:LIVE_MAX, at], jnp.zeros((PAD, 128), BF16), qr[:HALF, at], qm[HALF:LIVE_MAX, at]],
            axis=0,
        )
        value = values[:, at]
        mixed, fades = [], []
        for side in range(2):
            head = 2 * pair + side
            inside_q = (lane_q // HD) == side
            hot = jnp.where(lane_q == (1 - side) * HD, 1.0, 0.0).astype(BF16)
            q = jnp.where(inside_q, query, hot)
            k = jnp.where((lane_k // HD) == side, keys[:, at], shut)
            scores = dot(q, k, ((1,), (1,)))
            top = jnp.max(scores, axis=1, keepdims=True)
            if not first_call:
                old_top = stats[:, head : head + 1]
                top = jnp.maximum(top, old_top)
                fade = jnp.exp2((old_top - top) * RATE)
                fades.append(fade)
            weights = jnp.exp2((scores - top) * RATE)
            total = jnp.sum(weights, axis=1, keepdims=True)
            if not first_call:
                total = total + stats[:, heads + head : heads + head + 1] * fade
            stats = jnp.where(lane_a == head, top, stats)
            stats = jnp.where(lane_a == heads + head, total, stats)
            mixed.append(dot(weights.astype(BF16), value))
        inside = lane_a < HD
        merged = jnp.where(inside, mixed[0], mixed[1])
        if not first_call:
            merged = merged + state_ref[:, at] * jnp.where(inside, fades[0], fades[1])
        out_ref[:, at] = merged
    out_ref[:, channels:] = stats


def attend(qm, qr, own, first, second, gain, wk, wv, state=None):
    channels = own.shape[1]
    args = [qm, qr, own, first, second, gain, wk, wv] + ([] if state is None else [state])
    keys = 2 * LIVE_MAX
    return pl.pallas_call(
        functools.partial(attend_kernel, state is None),
        in_specs=vmem(len(args)),
        out_specs=pl.BlockSpec(memory_space=pltpu.VMEM),
        out_shape=jax.ShapeDtypeStruct((QROWS, channels + 128), F32),
        input_output_aliases={} if state is None else {len(args) - 1: 0},
        compiler_params=params(),
        cost_estimate=pl.CostEstimate(
            flops=2 * 10**9, bytes_accessed=4 * 10**6, transcendentals=QROWS * keys * channels // HD
        ),
        name="attend",
    )(*args)


def combine_kernel(mine_ref, other_ref, out_ref):
    rows, width = other_ref.shape
    channels = width - 128
    heads = channels // HD
    lane = lax.broadcasted_iota(jnp.int32, (rows, 128), 1)

    def theirs(at):
        return jnp.concatenate([other_ref[PAD:, at], other_ref[:PAD, at]], axis=0)

    mine_stats = mine_ref[:rows, channels:]
    other_stats = theirs(slice(channels, width))
    for pair in range(heads // 2):
        at = slice(pair * 128, (pair + 1) * 128)
        scale_mine, scale_other = [], []
        for head in (2 * pair, 2 * pair + 1):
            a, b = mine_stats[:, head : head + 1], other_stats[:, head : head + 1]
            top = jnp.maximum(a, b)
            a, b = jnp.exp2((a - top) * RATE), jnp.exp2((b - top) * RATE)
            total = (
                mine_stats[:, heads + head : heads + head + 1] * a
                + other_stats[:, heads + head : heads + head + 1] * b
            )
            scale_mine.append(a / total)
            scale_other.append(b / total)
        inside = lane < HD
        out_ref[:, at] = (
            mine_ref[:rows, at] * jnp.where(inside, scale_mine[0], scale_mine[1])
            + theirs(at) * jnp.where(inside, scale_other[0], scale_other[1])
        ).astype(BF16)


def combine(mine, other):
    rows = other.shape[0]
    return pl.pallas_call(
        combine_kernel,
        in_specs=vmem(2),
        out_specs=pl.BlockSpec(memory_space=pltpu.VMEM),
        out_shape=jax.ShapeDtypeStruct((rows, other.shape[1] - 128), BF16),
        compiler_params=params(),
        name="combine",
    )(mine, other)


def own_branch_kernel(attended_ref, w_ref, out_ref):
    out_ref[...] = dot(attended_ref[...], w_ref[lax.axis_index("head")])


def own_branch(attended, w_out):
    return pl.pallas_call(
        own_branch_kernel,
        in_specs=vmem(2),
        out_specs=pl.BlockSpec(memory_space=pltpu.VMEM),
        out_shape=jax.ShapeDtypeStruct((attended.shape[0], w_out.shape[2]), F32),
        compiler_params=params(),
        cost_estimate=pl.CostEstimate(flops=10**8, bytes_accessed=10**6, transcendentals=0),
        name="own_branch",
    )(attended, w_out)


def finish_kernel(branch_ref, attended_ref, w_ref, normed_ref, swapped_ref, out_ref):
    core = lax.rem(lax.axis_index("ctx"), 2)
    branch = branch_ref[...] + dot(attended_ref[...], w_ref[1 - lax.axis_index("head")])
    near = (branch[:HALF] + normed_ref[...].astype(F32)).astype(BF16)
    far = (branch[HALF:LIVE_MAX] + swapped_ref[LIVE_MAX:, :].astype(F32)).astype(BF16)
    even = jnp.where(core == 0, near, far)
    odd = jnp.where(core == 0, far, near)
    for block in range(HALF // 16):
        out_ref[32 * block : 32 * block + 16, :] = even[16 * block : 16 * block + 16]
        out_ref[32 * block + 16 : 32 * block + 32, :] = odd[16 * block : 16 * block + 16]
    rest = out_ref.shape[0] - LIVE_MAX
    out_ref[LIVE_MAX:, :] = jnp.broadcast_to(branch[LIVE_MAX : LIVE_MAX + 1], (rest, branch.shape[1])).astype(BF16)


def finish(branch, attended, w_out, normed, swapped):
    return pl.pallas_call(
        finish_kernel,
        in_specs=vmem(5),
        out_specs=pl.BlockSpec(memory_space=pltpu.VMEM),
        out_shape=jax.ShapeDtypeStruct((ANCH_DEV, branch.shape[1]), BF16),
        compiler_params=params(),
        name="finish",
    )(branch, attended, w_out, normed, swapped)


def pairs(move):
    found = []
    for z in range(4):
        for y in range(2):
            for core in range(2):
                for x in range(2):
                    to_z, to_y, to_core, to_x = move(z, y, core, x)
                    found.append((((z * 2 + y) * 2 + core) * 2 + x, ((to_z * 2 + to_y) * 2 + to_core) * 2 + to_x))
    return found


def send(array, move):
    return lax.ppermute(array, ALL, pairs(move))


def across_core(z, y, core, x):
    return z, y, 1 - core, x


def across_x(z, y, core, x):
    return z, y, core, 1 - x


def across_first(z, y, core, x):
    return (z, 1 - y, core, x) if core == 0 else (z, y, core, 1 - x)


def across_second(z, y, core, x):
    return (z, 1 - y, core, x) if core == 1 else (z, y, core, 1 - x)


def across_z(step):
    return lambda z, y, core, x: (z ^ step, y, core, x)


def halves(w):
    return w.reshape(2, w.shape[0] // 2, w.shape[1])


def block_plan(messages, node_anchor, anchor_count, norm_gain, w_query, w_key, w_value, w_out):
    channels = messages.shape[1]
    before, own, after = pool(messages, node_anchor)
    from_next = shift(before, -1)
    from_previous = shift(after, 1)
    keep, away = settle(anchor_count, own, from_next, from_previous)
    mine = jnp.concatenate([keep, send(away, across_core)], axis=0)
    slices = [mine] + [send(mine, across_z(step)) for step in (1, 2, 3)]
    gain = norm_gain.reshape(2, 1, channels)
    wq, wk, wv, wo = halves(w_query), halves(w_key), halves(w_value), halves(w_out)
    state = None
    for index, rows in enumerate(slices):
        first = send(rows, across_first)
        second = send(jnp.concatenate([rows, first], axis=0), across_second)
        if index == 0:
            swap, normed = make_queries(rows, first, second, gain, wq)
            swapped = send(swap, across_core)
        state = attend(swap, swapped, rows, first, second, gain, wk, wv, state)
    other = send(state[LIVE_MAX:], across_core)
    attended = combine(state, other)
    attended_other = send(attended, across_x)
    branch = own_branch(attended, wo)
    return finish(branch, attended_other, wo, normed, swapped)


def shift(x, by):
    peers = lax.axis_size("ctx")
    return lax.ppermute(x, "ctx", [(i, (i + by) % peers) for i in range(peers)])


def pool_local(messages, node_anchor, center):
    partitions = lax.axis_size("ctx")
    owner_dev = node_anchor // ANCH_DEV
    offset = (owner_dev - center + 1 + partitions) % partitions
    local_slot = node_anchor % ANCH_DEV
    channel_count = messages.shape[1]
    tile_count = messages.shape[0] // 128
    group = math.gcd(tile_count, 4)
    steps_count = tile_count // group
    slot_blocks = local_slot.reshape(steps_count, group, 128)
    offset_blocks = offset.reshape(steps_count, group, 128)[:, :, 0]
    message_blocks = messages.reshape(steps_count, group, 128, channel_count)
    columns = jnp.arange(ANCH_DEV, dtype=jnp.int32)

    def add_block(running, pieces):
        slot_block, offset_block, message_block = pieces
        onehot = (slot_block[:, :, None] == columns[None, None, :]).astype(jnp.bfloat16)
        partial_value = jnp.einsum(
            "tnk,tnc->tkc", onehot, message_block, preferred_element_type=jnp.float32
        )
        for tile in range(group):
            where = offset_block[tile]
            current = lax.dynamic_index_in_dim(running, where, 0, keepdims=False)
            running = lax.dynamic_update_index_in_dim(
                running, current + partial_value[tile], where, 0
            )
        return (running, None)

    initial = jnp.zeros((3, ANCH_DEV, channel_count), jnp.float32)
    running, unused = lax.scan(add_block, initial, (slot_blocks, offset_blocks, message_blocks))
    return running


def make_fold(queries, shard_rows, scale):
    heads_local = queries.shape[1]

    def fold(carry, pieces, start_row):
        key_rows, value_rows, live_rows = pieces
        shards = live_rows.shape[0] // shard_rows
        key_blocks = key_rows.reshape(shards, shard_rows, heads_local, HD)
        value_blocks = value_rows.reshape(shards, shard_rows, heads_local, HD)
        live_blocks = live_rows.reshape(shards, shard_rows)

        def visit(state, block):
            highest, totals, accum = state
            key_block, value_block, live_block = block
            scores = (
                jnp.einsum("qhd,khd->hqk", queries, key_block, preferred_element_type=jnp.float32)
                * scale
            )
            alive = (live_block > 0)[None, None, :]
            scores = jnp.where(alive, scores, NEG)
            newest = jnp.maximum(highest, jnp.max(scores, axis=-1))
            weights = jnp.where(alive, jnp.exp(scores - newest[..., None]), 0.0)
            factor = jnp.exp(highest - newest)
            totals = totals * factor + jnp.sum(weights, axis=-1)
            mixed = jnp.einsum(
                "hqk,khd->hqd",
                weights.astype(jnp.bfloat16),
                value_block,
                preferred_element_type=jnp.float32,
            )
            accum = accum * factor[..., None] + mixed
            return ((newest, totals, accum), None)

        carry, unused = lax.scan(visit, carry, (key_blocks, value_blocks, live_blocks))
        return carry

    return fold


def general_plan(messages, node_anchor, anchor_count, norm_gain, w_query, w_key, w_value, w_out):
    center = lax.axis_index("ctx")
    pooled_terms = pool_local(messages, node_anchor, center)
    for_previous = pooled_terms[0]
    own_rows = pooled_terms[1]
    for_next = pooled_terms[2]
    from_next = shift(for_previous, -1)
    from_previous = shift(for_next, 1)
    sums = own_rows + from_next + from_previous
    pooled = sums.astype(jnp.bfloat16)
    whole = lax.all_gather(pooled, "head", axis=1, tiled=True).astype(jnp.float32)
    mean_square = jnp.mean(whole * whole, axis=1, keepdims=True)
    normed = (whole * lax.rsqrt(mean_square + EPS) * norm_gain).astype(jnp.bfloat16)
    channel_count = messages.shape[1]
    local_normed = lax.dynamic_slice_in_dim(
        normed, lax.axis_index("head") * channel_count, channel_count, 1
    )
    heads_local = w_query.shape[1] // HD
    queries = jnp.dot(normed, w_query, preferred_element_type=jnp.float32).astype(jnp.bfloat16)
    keys_local = jnp.dot(normed, w_key, preferred_element_type=jnp.float32).astype(jnp.bfloat16)
    values_local = jnp.dot(normed, w_value, preferred_element_type=jnp.float32).astype(jnp.bfloat16)
    queries = queries.reshape(ANCH_DEV, heads_local, HD)
    scale = HD ** (-0.5)
    initial = (
        jnp.full((heads_local, ANCH_DEV), NEG, jnp.float32),
        jnp.zeros((heads_local, ANCH_DEV), jnp.float32),
        jnp.zeros((heads_local, ANCH_DEV, HD), jnp.float32),
    )
    live_flags = (jnp.arange(ANCH_DEV, dtype=jnp.int32) < anchor_count[0]).astype(jnp.bfloat16)
    fold = make_fold(queries, ANCH_DEV, scale)
    highest, totals, accum = fold(
        initial,
        (
            lax.all_gather(keys_local, "ctx", axis=0, tiled=True),
            lax.all_gather(values_local, "ctx", axis=0, tiled=True),
            lax.all_gather(live_flags, "ctx", axis=0, tiled=True),
        ),
        jnp.int32(0),
    )
    attended = (
        (accum / totals[..., None])
        .transpose(1, 0, 2)
        .reshape(ANCH_DEV, heads_local * HD)
        .astype(jnp.bfloat16)
    )
    branch = jnp.dot(
        lax.all_gather(attended, "head", axis=1, tiled=True),
        w_out,
        preferred_element_type=jnp.float32,
    )
    return (local_normed.astype(jnp.float32) + branch).astype(jnp.bfloat16)


def solution(mesh):
    placed = (
        P("ctx", "head"),
        P("ctx"),
        P("ctx"),
        P(),
        P(None, "head"),
        P(None, "head"),
        P(None, "head"),
        P(None, "head"),
    )
    sizes = (mesh.shape["ctx"], mesh.shape["head"])
    plan = block_plan if sizes == (16, 2) else general_plan
    return jax.shard_map(plan, mesh=mesh, in_specs=placed, out_specs=P("ctx", "head"), check_vma=False)
```

```python
import functools
import math

import jax
import jax.numpy as jnp
from jax import lax
from jax.experimental import pallas as pl
from jax.experimental.pallas import tpu as pltpu
from jax.sharding import PartitionSpec as P

HD = 64
ANCH_DEV = 256
LIVE_MAX = 192
HALF = LIVE_MAX // 2
PAD = 16
QROWS = 2 * LIVE_MAX
SPILL = 128 - HALF
TILE = 128

EPS = 1e-06
NEG = -1e30
MARK = 2.0**100
MARKED = 2.0**90
RATE = HD**-0.5 * math.log2(math.e)

ALL = ("ctx", "head")
F32 = jnp.float32
BF16 = jnp.bfloat16


def params(mib=32):
    return pltpu.CompilerParams(vmem_limit_bytes=mib * 2**20)


def vmem(count):
    return [pl.BlockSpec(memory_space=pltpu.VMEM)] * count


def dot(a, b, contract=((1,), (0,))):
    return lax.dot_general(a, b, (contract, ((), ())), preferred_element_type=F32)


def row_of(slot):
    block = slot // 16
    return (block % 2) * HALF + (block // 2) * 16 + slot % 16


def pool_kernel(tiles, anchors_smem, anchors_ref, messages_ref, before_ref, own_ref, after_ref, sums):
    step = pl.program_id(0)
    partitions = lax.axis_size("ctx")
    center = lax.axis_index("ctx")

    @pl.when(step == 0)
    def _():
        sums[...] = jnp.zeros_like(sums)

    rows = lax.broadcasted_iota(jnp.int32, (LIVE_MAX, TILE), 0)
    for tile in range(tiles):
        index = step * tiles + tile
        owner = anchors_smem[index * TILE] // ANCH_DEV
        side = lax.rem(owner - center + 1 + partitions, partitions)
        slot = row_of(anchors_ref[pl.ds(index, 1), :] % ANCH_DEV)
        onehot = jnp.where(rows == slot, 1.0, 0.0).astype(BF16)
        part = dot(onehot, messages_ref[tile * TILE : (tile + 1) * TILE, :])
        sums[side] += part

    @pl.when(step == pl.num_programs(0) - 1)
    def _():
        before_ref[...] = sums[0]
        own_ref[...] = sums[1]
        after_ref[...] = sums[2]


def pool(messages, node_anchor):
    nodes, channels = messages.shape
    steps = 8
    tiles = nodes // TILE // steps
    shape = jax.ShapeDtypeStruct((LIVE_MAX, channels), F32)
    whole = pl.BlockSpec((LIVE_MAX, channels), lambda i, a: (0, 0))
    return pl.pallas_call(
        functools.partial(pool_kernel, tiles),
        grid_spec=pltpu.PrefetchScalarGridSpec(
            num_scalar_prefetch=1,
            grid=(steps,),
            in_specs=[
                pl.BlockSpec((nodes // TILE, TILE), lambda i, a: (0, 0)),
                pl.BlockSpec((tiles * TILE, channels), lambda i, a: (i, 0)),
            ],
            out_specs=[whole] * 3,
            scratch_shapes=[pltpu.VMEM((3, LIVE_MAX, channels), F32)],
        ),
        out_shape=[shape] * 3,
        compiler_params=params(),
        name="pool",
    )(node_anchor, node_anchor.reshape(nodes // TILE, TILE), messages)


def settle_kernel(count_ref, own_ref, before_ref, after_ref, keep_ref, send_ref):
    core = lax.rem(lax.axis_index("ctx"), 2)
    count = count_ref[0]

    def half(which):
        at = pl.ds(pl.multiple_of(which * HALF, 16), HALF)
        total = own_ref[at, :] + before_ref[at, :] + after_ref[at, :]
        row = lax.broadcasted_iota(jnp.int32, total.shape, 0)
        slot = (2 * (row // 16) + which) * 16 + row % 16
        return jnp.where(slot < count, total, MARK).astype(BF16)

    keep_ref[...] = half(core)
    send_ref[...] = half(1 - core)


def settle(count, own, before, after):
    channels = own.shape[1]
    shape = jax.ShapeDtypeStruct((HALF, channels), BF16)
    return pl.pallas_call(
        settle_kernel,
        in_specs=[pl.BlockSpec(memory_space=pltpu.SMEM)] + vmem(3),
        out_specs=vmem(2),
        out_shape=[shape] * 2,
        compiler_params=params(),
        name="settle",
    )(count, own, before, after)


def normalise(mine, other, gain_ref, x):
    channels = mine.shape[1]
    mine, other = mine.astype(F32), other.astype(F32)
    dead = mine[:, :1] > MARKED
    mine = jnp.where(dead, 0.0, mine)
    other = jnp.where(dead, 0.0, other)
    square = jnp.sum(mine * mine + other * other, axis=1, keepdims=True)
    inverse = lax.rsqrt(square * (1.0 / (2 * channels)) + EPS)
    mine = (mine * inverse * gain_ref[x]).astype(BF16)
    other = (other * inverse * gain_ref[1 - x]).astype(BF16)
    return mine, other, dead


def project(mine, other, w_ref, x):
    return (dot(mine, w_ref[x]) + dot(other, w_ref[1 - x])).astype(BF16)


def query_kernel(own_ref, first_ref, second_ref, gain_ref, wq_ref, swap_ref, normed_ref):
    core = lax.rem(lax.axis_index("ctx"), 2)
    x = lax.axis_index("head")
    other = jnp.where(core == 0, second_ref[:LIVE_MAX, :], first_ref[...])
    mine, other, unused = normalise(own_ref[...], other, gain_ref, x)
    swap_ref[:LIVE_MAX, :] = project(mine, other, wq_ref, x)
    swap_ref[LIVE_MAX:, :] = mine[HALF:]
    normed_ref[...] = mine[:HALF]


def make_queries(own, first, second, gain, wq):
    channels = own.shape[1]
    return pl.pallas_call(
        query_kernel,
        in_specs=vmem(5),
        out_specs=vmem(2),
        out_shape=[
            jax.ShapeDtypeStruct((LIVE_MAX + HALF, channels), BF16),
            jax.ShapeDtypeStruct((HALF, channels), BF16),
        ],
        compiler_params=params(),
        cost_estimate=pl.CostEstimate(flops=4 * 10**8, bytes_accessed=2 * 10**6, transcendentals=0),
        name="queries",
    )(own, first, second, gain, wq)


def attend_kernel(first_call, *refs):
    if first_call:
        qm, qr, own_ref, first_ref, second_ref, gain_ref, wk_ref, wv_ref, out_ref = refs
        state_ref = None
    else:
        qm, qr, own_ref, first_ref, second_ref, gain_ref, wk_ref, wv_ref, state_ref, out_ref = refs
    core = lax.rem(lax.axis_index("ctx"), 2)
    x = lax.axis_index("head")
    channels = own_ref.shape[1]
    heads = channels // HD
    one, two = first_ref[...], second_ref[:LIVE_MAX, :]
    mine = jnp.concatenate([own_ref[...], jnp.where(core == 0, one, two)], axis=0)
    other = jnp.concatenate([jnp.where(core == 0, two, one), second_ref[LIVE_MAX:, :]], axis=0)
    mine, other, dead = normalise(mine, other, gain_ref, x)
    keys = project(mine, other, wk_ref, x)
    values = project(mine, other, wv_ref, x).T
    shut = jnp.where(dead, NEG, 0.0).astype(BF16)

    live = jnp.sum(jnp.where(dead, 0.0, 1.0), axis=0, keepdims=True)
    value_sum = jnp.sum(values.astype(F32), axis=1, keepdims=True)
    if not first_call:
        live = live + state_ref[channels + 2 * heads : channels + 2 * heads + 1, QROWS : QROWS + 1]
        value_sum = value_sum + state_ref[:channels, QROWS : QROWS + 1]
    out_ref[:channels, QROWS:] = jnp.broadcast_to(value_sum, (channels, 128))
    out_ref[channels:, QROWS:] = jnp.broadcast_to(live, (out_ref.shape[0] - channels, 128))

    lane_k = lax.broadcasted_iota(jnp.int32, (keys.shape[0], 128), 1)
    lane_q = lax.broadcasted_iota(jnp.int32, (QROWS, 128), 1)
    for pair in range(heads // 2):
        at = slice(pair * 128, (pair + 1) * 128)
        query = jnp.concatenate(
            [qm[:HALF, at], qr[HALF:LIVE_MAX, at], qm[HALF + SPILL : LIVE_MAX, at], qr[:HALF, at], qm[HALF : HALF + SPILL, at]],
            axis=0,
        )
        for side in range(2):
            head = 2 * pair + side
            hot = jnp.where(lane_q == (1 - side) * HD, 1.0, 0.0).astype(BF16)
            q = jnp.where((lane_q // HD) == side, query, hot)
            k = jnp.where((lane_k // HD) == side, keys[:, at], shut)
            scores = dot(k, q, ((1,), (1,)))
            top = jnp.max(scores, axis=0, keepdims=True)
            at_top = slice(channels + head, channels + head + 1)
            at_total = slice(channels + heads + head, channels + heads + head + 1)
            if not first_call:
                old_top = state_ref[at_top, :QROWS]
                top = jnp.maximum(top, old_top)
                fade = jnp.exp2((old_top - top) * RATE)
            weights = jnp.exp2((scores - top) * RATE)
            total = jnp.sum(weights, axis=0, keepdims=True)
            at_head = slice(head * HD, (head + 1) * HD)
            mixed = dot(values[at_head], weights.astype(BF16))
            if not first_call:
                total = total + state_ref[at_total, :QROWS] * fade
                mixed = mixed + state_ref[at_head, :QROWS] * fade
            out_ref[at_head, :QROWS] = mixed
            out_ref[at_top, :QROWS] = top
            out_ref[at_total, :QROWS] = total


def attend(qm, qr, own, first, second, gain, wk, wv, state=None):
    channels = own.shape[1]
    args = [qm, qr, own, first, second, gain, wk, wv] + ([] if state is None else [state])
    keys = 2 * LIVE_MAX
    return pl.pallas_call(
        functools.partial(attend_kernel, state is None),
        in_specs=vmem(len(args)),
        out_specs=pl.BlockSpec(memory_space=pltpu.VMEM),
        out_shape=jax.ShapeDtypeStruct((channels + 2 * (channels // HD) + 8, QROWS + 128), F32),
        input_output_aliases={} if state is None else {len(args) - 1: 0},
        compiler_params=params(),
        cost_estimate=pl.CostEstimate(
            flops=2 * 10**9, bytes_accessed=4 * 10**6, transcendentals=QROWS * keys * channels // HD
        ),
        name="attend",
    )(*args)


def combine_kernel(mine_ref, other_ref, out_ref):
    channels = out_ref.shape[1]
    heads = channels // HD
    width = 256
    lane = lax.broadcasted_iota(jnp.int32, (HD, width), 1)

    def theirs(at):
        middle = other_ref[at, :128]
        return jnp.concatenate([other_ref[at, 128:256], middle[:, 64:], middle[:, :64]], axis=1)

    at = slice(channels + 2 * heads, channels + 2 * heads + 1)
    live = mine_ref[at, QROWS : QROWS + 1] + other_ref[at, 256:257]
    for head in range(heads):
        at_top = slice(channels + head, channels + head + 1)
        at_total = slice(channels + heads + head, channels + heads + head + 1)
        at = slice(head * HD, (head + 1) * HD)
        a, b = mine_ref[at_top, :width], theirs(at_top)
        top = jnp.maximum(a, b)
        a, b = jnp.exp2((a - top) * RATE), jnp.exp2((b - top) * RATE)
        total = mine_ref[at_total, :width] * a + theirs(at_total) * b
        mixed = (mine_ref[at, :width] * a + theirs(at) * b) / total
        mean = (mine_ref[at, QROWS : QROWS + 1] + other_ref[at, 256:257]) / live
        mixed = jnp.where(lane < LIVE_MAX, mixed, mean)
        out_ref[:, at] = mixed.T[: LIVE_MAX + PAD].astype(BF16)


def combine(mine, other):
    channels = other.shape[0] // (HD + 2) * HD
    return pl.pallas_call(
        combine_kernel,
        in_specs=vmem(2),
        out_specs=pl.BlockSpec(memory_space=pltpu.VMEM),
        out_shape=jax.ShapeDtypeStruct((LIVE_MAX + PAD, channels), BF16),
        compiler_params=params(),
        name="combine",
    )(mine, other)


def own_branch_kernel(attended_ref, w_ref, out_ref):
    out_ref[...] = dot(attended_ref[...], w_ref[lax.axis_index("head")])


def own_branch(attended, w_out):
    return pl.pallas_call(
        own_branch_kernel,
        in_specs=vmem(2),
        out_specs=pl.BlockSpec(memory_space=pltpu.VMEM),
        out_shape=jax.ShapeDtypeStruct((attended.shape[0], w_out.shape[2]), F32),
        compiler_params=params(),
        cost_estimate=pl.CostEstimate(flops=10**8, bytes_accessed=10**6, transcendentals=0),
        name="own_branch",
    )(attended, w_out)


def finish_kernel(branch_ref, attended_ref, w_ref, normed_ref, swapped_ref, out_ref):
    core = lax.rem(lax.axis_index("ctx"), 2)
    branch = branch_ref[...] + dot(attended_ref[...], w_ref[1 - lax.axis_index("head")])
    near = (branch[:HALF] + normed_ref[...].astype(F32)).astype(BF16)
    far = (branch[HALF:LIVE_MAX] + swapped_ref[LIVE_MAX:, :].astype(F32)).astype(BF16)
    even = jnp.where(core == 0, near, far)
    odd = jnp.where(core == 0, far, near)
    for block in range(HALF // 16):
        out_ref[32 * block : 32 * block + 16, :] = even[16 * block : 16 * block + 16]
        out_ref[32 * block + 16 : 32 * block + 32, :] = odd[16 * block : 16 * block + 16]
    rest = out_ref.shape[0] - LIVE_MAX
    out_ref[LIVE_MAX:, :] = jnp.broadcast_to(branch[LIVE_MAX : LIVE_MAX + 1], (rest, branch.shape[1])).astype(BF16)


def finish(branch, attended, w_out, normed, swapped):
    return pl.pallas_call(
        finish_kernel,
        in_specs=vmem(5),
        out_specs=pl.BlockSpec(memory_space=pltpu.VMEM),
        out_shape=jax.ShapeDtypeStruct((ANCH_DEV, branch.shape[1]), BF16),
        compiler_params=params(),
        name="finish",
    )(branch, attended, w_out, normed, swapped)


def pairs(move):
    found = []
    for z in range(4):
        for y in range(2):
            for core in range(2):
                for x in range(2):
                    to_z, to_y, to_core, to_x = move(z, y, core, x)
                    found.append((((z * 2 + y) * 2 + core) * 2 + x, ((to_z * 2 + to_y) * 2 + to_core) * 2 + to_x))
    return found


def send(array, move):
    return lax.ppermute(array, ALL, pairs(move))


def across_core(z, y, core, x):
    return z, y, 1 - core, x


def across_x(z, y, core, x):
    return z, y, core, 1 - x


def across_first(z, y, core, x):
    return (z, 1 - y, core, x) if core == 0 else (z, y, core, 1 - x)


def across_second(z, y, core, x):
    return (z, 1 - y, core, x) if core == 1 else (z, y, core, 1 - x)


def across_z(step):
    return lambda z, y, core, x: (z ^ step, y, core, x)


def halves(w):
    return w.reshape(2, w.shape[0] // 2, w.shape[1])


def block_plan(messages, node_anchor, anchor_count, norm_gain, w_query, w_key, w_value, w_out):
    channels = messages.shape[1]
    before, own, after = pool(messages, node_anchor)
    from_next = shift(before, -1)
    from_previous = shift(after, 1)
    keep, away = settle(anchor_count, own, from_next, from_previous)
    mine = jnp.concatenate([keep, send(away, across_core)], axis=0)
    slices = [mine] + [send(mine, across_z(step)) for step in (1, 2, 3)]
    gain = norm_gain.reshape(2, 1, channels)
    wq, wk, wv, wo = halves(w_query), halves(w_key), halves(w_value), halves(w_out)
    state = None
    for index, rows in enumerate(slices):
        first = send(rows, across_first)
        second = send(jnp.concatenate([rows, first], axis=0), across_second)
        if index == 0:
            swap, normed = make_queries(rows, first, second, gain, wq)
            swapped = send(swap, across_core)
        state = attend(swap, swapped, rows, first, second, gain, wk, wv, state)
    other = send(state[:, 128:], across_core)
    attended = combine(state, other)
    attended_other = send(attended, across_x)
    branch = own_branch(attended, wo)
    return finish(branch, attended_other, wo, normed, swapped)


def shift(x, by):
    peers = lax.axis_size("ctx")
    return lax.ppermute(x, "ctx", [(i, (i + by) % peers) for i in range(peers)])


def pool_local(messages, node_anchor, center):
    partitions = lax.axis_size("ctx")
    owner_dev = node_anchor // ANCH_DEV
    offset = (owner_dev - center + 1 + partitions) % partitions
    local_slot = node_anchor % ANCH_DEV
    channel_count = messages.shape[1]
    tile_count = messages.shape[0] // 128
    group = math.gcd(tile_count, 4)
    steps_count = tile_count // group
    slot_blocks = local_slot.reshape(steps_count, group, 128)
    offset_blocks = offset.reshape(steps_count, group, 128)[:, :, 0]
    message_blocks = messages.reshape(steps_count, group, 128, channel_count)
    columns = jnp.arange(ANCH_DEV, dtype=jnp.int32)

    def add_block(running, pieces):
        slot_block, offset_block, message_block = pieces
        onehot = (slot_block[:, :, None] == columns[None, None, :]).astype(jnp.bfloat16)
        partial_value = jnp.einsum(
            "tnk,tnc->tkc", onehot, message_block, preferred_element_type=jnp.float32
        )
        for tile in range(group):
            where = offset_block[tile]
            current = lax.dynamic_index_in_dim(running, where, 0, keepdims=False)
            running = lax.dynamic_update_index_in_dim(
                running, current + partial_value[tile], where, 0
            )
        return (running, None)

    initial = jnp.zeros((3, ANCH_DEV, channel_count), jnp.float32)
    running, unused = lax.scan(add_block, initial, (slot_blocks, offset_blocks, message_blocks))
    return running


def make_fold(queries, shard_rows, scale):
    heads_local = queries.shape[1]

    def fold(carry, pieces, start_row):
        key_rows, value_rows, live_rows = pieces
        shards = live_rows.shape[0] // shard_rows
        key_blocks = key_rows.reshape(shards, shard_rows, heads_local, HD)
        value_blocks = value_rows.reshape(shards, shard_rows, heads_local, HD)
        live_blocks = live_rows.reshape(shards, shard_rows)

        def visit(state, block):
            highest, totals, accum = state
            key_block, value_block, live_block = block
            scores = (
                jnp.einsum("qhd,khd->hqk", queries, key_block, preferred_element_type=jnp.float32)
                * scale
            )
            alive = (live_block > 0)[None, None, :]
            scores = jnp.where(alive, scores, NEG)
            newest = jnp.maximum(highest, jnp.max(scores, axis=-1))
            weights = jnp.where(alive, jnp.exp(scores - newest[..., None]), 0.0)
            factor = jnp.exp(highest - newest)
            totals = totals * factor + jnp.sum(weights, axis=-1)
            mixed = jnp.einsum(
                "hqk,khd->hqd",
                weights.astype(jnp.bfloat16),
                value_block,
                preferred_element_type=jnp.float32,
            )
            accum = accum * factor[..., None] + mixed
            return ((newest, totals, accum), None)

        carry, unused = lax.scan(visit, carry, (key_blocks, value_blocks, live_blocks))
        return carry

    return fold


def general_plan(messages, node_anchor, anchor_count, norm_gain, w_query, w_key, w_value, w_out):
    center = lax.axis_index("ctx")
    pooled_terms = pool_local(messages, node_anchor, center)
    for_previous = pooled_terms[0]
    own_rows = pooled_terms[1]
    for_next = pooled_terms[2]
    from_next = shift(for_previous, -1)
    from_previous = shift(for_next, 1)
    sums = own_rows + from_next + from_previous
    pooled = sums.astype(jnp.bfloat16)
    whole = lax.all_gather(pooled, "head", axis=1, tiled=True).astype(jnp.float32)
    mean_square = jnp.mean(whole * whole, axis=1, keepdims=True)
    normed = (whole * lax.rsqrt(mean_square + EPS) * norm_gain).astype(jnp.bfloat16)
    channel_count = messages.shape[1]
    local_normed = lax.dynamic_slice_in_dim(
        normed, lax.axis_index("head") * channel_count, channel_count, 1
    )
    heads_local = w_query.shape[1] // HD
    queries = jnp.dot(normed, w_query, preferred_element_type=jnp.float32).astype(jnp.bfloat16)
    keys_local = jnp.dot(normed, w_key, preferred_element_type=jnp.float32).astype(jnp.bfloat16)
    values_local = jnp.dot(normed, w_value, preferred_element_type=jnp.float32).astype(jnp.bfloat16)
    queries = queries.reshape(ANCH_DEV, heads_local, HD)
    scale = HD ** (-0.5)
    initial = (
        jnp.full((heads_local, ANCH_DEV), NEG, jnp.float32),
        jnp.zeros((heads_local, ANCH_DEV), jnp.float32),
        jnp.zeros((heads_local, ANCH_DEV, HD), jnp.float32),
    )
    live_flags = (jnp.arange(ANCH_DEV, dtype=jnp.int32) < anchor_count[0]).astype(jnp.bfloat16)
    fold = make_fold(queries, ANCH_DEV, scale)
    highest, totals, accum = fold(
        initial,
        (
            lax.all_gather(keys_local, "ctx", axis=0, tiled=True),
            lax.all_gather(values_local, "ctx", axis=0, tiled=True),
            lax.all_gather(live_flags, "ctx", axis=0, tiled=True),
        ),
        jnp.int32(0),
    )
    attended = (
        (accum / totals[..., None])
        .transpose(1, 0, 2)
        .reshape(ANCH_DEV, heads_local * HD)
        .astype(jnp.bfloat16)
    )
    branch = jnp.dot(
        lax.all_gather(attended, "head", axis=1, tiled=True),
        w_out,
        preferred_element_type=jnp.float32,
    )
    return (local_normed.astype(jnp.float32) + branch).astype(jnp.bfloat16)


def solution(mesh):
    placed = (
        P("ctx", "head"),
        P("ctx"),
        P("ctx"),
        P(),
        P(None, "head"),
        P(None, "head"),
        P(None, "head"),
        P(None, "head"),
    )
    sizes = (mesh.shape["ctx"], mesh.shape["head"])
    plan = block_plan if sizes == (16, 2) else general_plan
    return jax.shard_map(plan, mesh=mesh, in_specs=placed, out_specs=P("ctx", "head"), check_vma=False)
```

```python
import functools
import math

import jax
import jax.numpy as jnp
from jax import lax
from jax.experimental import pallas as pl
from jax.experimental.pallas import tpu as pltpu
from jax.sharding import PartitionSpec as P

HD = 64
ANCH_DEV = 256
LIVE_MAX = 192
PAD = 16
QROWS = 2 * LIVE_MAX
SENT = 256
TILE = 128

EPS = 1e-06
NEG = -1e30
MARK = 2.0**100
MARKED = 2.0**90
RATE = HD**-0.5 * math.log2(math.e)

ALL = ("ctx", "head")
F32 = jnp.float32
BF16 = jnp.bfloat16


def params(mib=32):
    return pltpu.CompilerParams(vmem_limit_bytes=mib * 2**20)


def vmem(count):
    return [pl.BlockSpec(memory_space=pltpu.VMEM)] * count


def dot(a, b, contract=((1,), (0,))):
    return lax.dot_general(a, b, (contract, ((), ())), preferred_element_type=F32)


def pool_kernel(tiles, anchors_smem, anchors_ref, messages_ref, before_ref, own_ref, after_ref, sums):
    step = pl.program_id(0)
    partitions = lax.axis_size("ctx")
    center = lax.axis_index("ctx")

    @pl.when(step == 0)
    def _():
        sums[...] = jnp.zeros_like(sums)

    rows = lax.broadcasted_iota(jnp.int32, (LIVE_MAX, TILE), 0)
    for tile in range(tiles):
        index = step * tiles + tile
        owner = anchors_smem[index * TILE] // ANCH_DEV
        side = lax.rem(owner - center + 1 + partitions, partitions)
        slot = anchors_ref[pl.ds(index, 1), :] % ANCH_DEV
        onehot = jnp.where(rows == slot, 1.0, 0.0).astype(BF16)
        part = dot(onehot, messages_ref[tile * TILE : (tile + 1) * TILE, :])
        sums[side] += part

    @pl.when(step == pl.num_programs(0) - 1)
    def _():
        before_ref[...] = sums[0]
        own_ref[...] = sums[1]
        after_ref[...] = sums[2]


def pool(messages, node_anchor):
    nodes, channels = messages.shape
    steps = 8
    tiles = nodes // TILE // steps
    shape = jax.ShapeDtypeStruct((LIVE_MAX, channels), F32)
    whole = pl.BlockSpec((LIVE_MAX, channels), lambda i, a: (0, 0))
    return pl.pallas_call(
        functools.partial(pool_kernel, tiles),
        grid_spec=pltpu.PrefetchScalarGridSpec(
            num_scalar_prefetch=1,
            grid=(steps,),
            in_specs=[
                pl.BlockSpec((nodes // TILE, TILE), lambda i, a: (0, 0)),
                pl.BlockSpec((tiles * TILE, channels), lambda i, a: (i, 0)),
            ],
            out_specs=[whole] * 3,
            scratch_shapes=[pltpu.VMEM((3, LIVE_MAX, channels), F32)],
        ),
        out_shape=[shape] * 3,
        compiler_params=params(60),
        name="pool",
    )(node_anchor, node_anchor.reshape(nodes // TILE, TILE), messages)


def settle_kernel(count_ref, own_ref, before_ref, after_ref, out_ref):
    total = own_ref[...] + before_ref[...] + after_ref[...]
    slot = lax.broadcasted_iota(jnp.int32, total.shape, 0)
    out_ref[...] = jnp.where(slot < count_ref[0], total, MARK).astype(BF16)


def settle(count, own, before, after):
    return pl.pallas_call(
        settle_kernel,
        in_specs=[pl.BlockSpec(memory_space=pltpu.SMEM)] + vmem(3),
        out_specs=pl.BlockSpec(memory_space=pltpu.VMEM),
        out_shape=jax.ShapeDtypeStruct(own.shape, BF16),
        compiler_params=params(),
        name="settle",
    )(count, own, before, after)


def join_kernel(a_ref, b_ref, *rest):
    rows = a_ref.shape[0]
    rest[-1][:rows, :] = a_ref[...]
    rest[-1][rows:, :] = b_ref[...]


def join(a, b, *after):
    return pl.pallas_call(
        join_kernel,
        in_specs=vmem(2) + [pl.BlockSpec(memory_space=pl.ANY)] * len(after),
        out_specs=pl.BlockSpec(memory_space=pltpu.VMEM),
        out_shape=jax.ShapeDtypeStruct((a.shape[0] + b.shape[0], a.shape[1]), a.dtype),
        compiler_params=params(),
        name="join",
    )(a, b, *after)


def normalise(mine, other, gain_ref, x):
    channels = mine.shape[1]
    mine, other = mine.astype(F32), other.astype(F32)
    dead = mine[:, :1] > MARKED
    mine = jnp.where(dead, 0.0, mine)
    other = jnp.where(dead, 0.0, other)
    square = jnp.sum(mine * mine + other * other, axis=1, keepdims=True)
    inverse = lax.rsqrt(square * (1.0 / (2 * channels)) + EPS)
    mine = (mine * inverse * gain_ref[x]).astype(BF16)
    other = (other * inverse * gain_ref[1 - x]).astype(BF16)
    return mine, other, dead


def project(mine, other, w_ref, x):
    return (dot(mine, w_ref[x]) + dot(other, w_ref[1 - x])).astype(BF16)


def query_kernel(own_ref, first_ref, second_ref, gain_ref, wq_ref, query_ref, normed_ref):
    core = lax.rem(lax.axis_index("ctx"), 2)
    x = lax.axis_index("head")
    other = jnp.where(core == 0, second_ref[:LIVE_MAX, :], first_ref[...])
    mine, other, unused = normalise(own_ref[...], other, gain_ref, x)
    query_ref[...] = project(mine, other, wq_ref, x)
    normed_ref[...] = mine


def make_queries(own, first, second, gain, wq):
    channels = own.shape[1]
    return pl.pallas_call(
        query_kernel,
        in_specs=vmem(5),
        out_specs=vmem(2),
        out_shape=[jax.ShapeDtypeStruct((LIVE_MAX, channels), BF16)] * 2,
        compiler_params=params(),
        cost_estimate=pl.CostEstimate(flops=4 * 10**8, bytes_accessed=2 * 10**6, transcendentals=0),
        name="queries",
    )(own, first, second, gain, wq)


def attend_kernel(first_call, *refs):
    if first_call:
        qm, qr, own_ref, first_ref, second_ref, gain_ref, wk_ref, wv_ref, out_ref = refs
        state_ref = None
    else:
        qm, qr, own_ref, first_ref, second_ref, gain_ref, wk_ref, wv_ref, state_ref, out_ref = refs
    core = lax.rem(lax.axis_index("ctx"), 2)
    x = lax.axis_index("head")
    channels = own_ref.shape[1]
    heads = channels // HD
    one, two = first_ref[...], second_ref[:LIVE_MAX, :]
    mine = jnp.concatenate([own_ref[...], jnp.where(core == 0, one, two)], axis=0)
    other = jnp.concatenate([jnp.where(core == 0, two, one), second_ref[LIVE_MAX:, :]], axis=0)
    mine, other, dead = normalise(mine, other, gain_ref, x)
    keys = project(mine, other, wk_ref, x)
    values = project(mine, other, wv_ref, x)
    shut = jnp.where(dead, NEG, 0.0).astype(BF16)

    live = jnp.sum(jnp.where(dead, 0.0, 1.0), axis=0, keepdims=True)
    live = jnp.broadcast_to(live, (1, SENT))
    value_sum = jnp.sum(values.astype(F32), axis=0, keepdims=True)
    extra = channels + 2 * heads
    for part in range(channels // SENT):
        at = value_sum[:, part * SENT : (part + 1) * SENT]
        row = slice(extra + part, extra + part + 1)
        out_ref[row, QROWS - SENT :] = at if first_call else at + state_ref[row, QROWS - SENT :]
    row = slice(extra + channels // SENT, extra + channels // SENT + 1)
    out_ref[row, QROWS - SENT :] = live if first_call else live + state_ref[row, QROWS - SENT :]
    values = values.T

    lane_k = lax.broadcasted_iota(jnp.int32, (keys.shape[0], 128), 1)
    lane_q = lax.broadcasted_iota(jnp.int32, (QROWS, 128), 1)
    for pair in range(heads // 2):
        at = slice(pair * 128, (pair + 1) * 128)
        query = jnp.concatenate(
            [qm[:, at], qr[128:, at], qr[:128, at]],
            axis=0,
        )
        for side in range(2):
            head = 2 * pair + side
            hot = jnp.where(lane_q == (1 - side) * HD, 1.0, 0.0).astype(BF16)
            q = jnp.where((lane_q // HD) == side, query, hot)
            k = jnp.where((lane_k // HD) == side, keys[:, at], shut)
            scores = dot(k, q, ((1,), (1,)))
            top = jnp.max(scores, axis=0, keepdims=True)
            at_top = slice(channels + head, channels + head + 1)
            at_total = slice(channels + heads + head, channels + heads + head + 1)
            if not first_call:
                old_top = state_ref[at_top, :QROWS]
                top = jnp.maximum(top, old_top)
                fade = jnp.exp2((old_top - top) * RATE)
            weights = jnp.exp2((scores - top) * RATE)
            total = jnp.sum(weights, axis=0, keepdims=True)
            at_head = slice(head * HD, (head + 1) * HD)
            mixed = dot(values[at_head], weights.astype(BF16))
            if not first_call:
                total = total + state_ref[at_total, :QROWS] * fade
                mixed = mixed + state_ref[at_head, :QROWS] * fade
            out_ref[at_head, :QROWS] = mixed
            out_ref[at_top, :QROWS] = top
            out_ref[at_total, :QROWS] = total


def attend(qm, qr, own, first, second, gain, wk, wv, state=None):
    channels = own.shape[1]
    args = [qm, qr, own, first, second, gain, wk, wv] + ([] if state is None else [state])
    keys = 2 * LIVE_MAX
    return pl.pallas_call(
        functools.partial(attend_kernel, state is None),
        in_specs=vmem(len(args)),
        out_specs=pl.BlockSpec(memory_space=pltpu.VMEM),
        out_shape=jax.ShapeDtypeStruct((channels + 2 * (channels // HD) + 8, QROWS), F32),
        input_output_aliases={} if state is None else {len(args) - 1: 0},
        compiler_params=params(),
        cost_estimate=pl.CostEstimate(
            flops=2 * 10**9, bytes_accessed=4 * 10**6, transcendentals=QROWS * keys * channels // HD
        ),
        name="attend",
    )(*args)


def combine_kernel(mine_ref, other_ref, out_ref):
    channels = out_ref.shape[1]
    heads = channels // HD

    def theirs(at):
        middle = other_ref[at, :128]
        return jnp.concatenate([other_ref[at, 128:], middle[:, 64:], middle[:, :64]], axis=1)

    for head in range(heads):
        at_top = slice(channels + head, channels + head + 1)
        at_total = slice(channels + heads + head, channels + heads + head + 1)
        at = slice(head * HD, (head + 1) * HD)
        a, b = mine_ref[at_top, :SENT], theirs(at_top)
        top = jnp.maximum(a, b)
        a, b = jnp.exp2((a - top) * RATE), jnp.exp2((b - top) * RATE)
        total = mine_ref[at_total, :SENT] * a + theirs(at_total) * b
        mixed = (mine_ref[at, :SENT] * a + theirs(at) * b) / total
        out_ref[:LIVE_MAX, at] = mixed.T[:LIVE_MAX].astype(BF16)
    extra = channels + 2 * heads
    sums = mine_ref[extra : extra + 8, QROWS - SENT :] + other_ref[extra : extra + 8, :]
    parts = channels // SENT
    live = sums[parts : parts + 1, :]
    for part in range(parts):
        mean = (sums[part : part + 1, :] / live).astype(BF16)
        out_ref[LIVE_MAX:, part * SENT : (part + 1) * SENT] = jnp.broadcast_to(mean, (PAD, SENT))


def combine(mine, other):
    channels = other.shape[0] // (HD + 2) * HD
    return pl.pallas_call(
        combine_kernel,
        in_specs=vmem(2),
        out_specs=pl.BlockSpec(memory_space=pltpu.VMEM),
        out_shape=jax.ShapeDtypeStruct((LIVE_MAX + PAD, channels), BF16),
        compiler_params=params(),
        name="combine",
    )(mine, other)


def own_branch_kernel(attended_ref, w_ref, out_ref):
    out_ref[...] = dot(attended_ref[...], w_ref[lax.axis_index("head")])


def own_branch(attended, w_out):
    return pl.pallas_call(
        own_branch_kernel,
        in_specs=vmem(2),
        out_specs=pl.BlockSpec(memory_space=pltpu.VMEM),
        out_shape=jax.ShapeDtypeStruct((attended.shape[0], w_out.shape[2]), F32),
        compiler_params=params(),
        cost_estimate=pl.CostEstimate(flops=10**8, bytes_accessed=10**6, transcendentals=0),
        name="own_branch",
    )(attended, w_out)


def finish_kernel(branch_ref, attended_ref, w_ref, normed_ref, out_ref):
    branch = branch_ref[...] + dot(attended_ref[...], w_ref[1 - lax.axis_index("head")])
    out_ref[:LIVE_MAX, :] = (branch[:LIVE_MAX] + normed_ref[...].astype(F32)).astype(BF16)
    rest = out_ref.shape[0] - LIVE_MAX
    out_ref[LIVE_MAX:, :] = jnp.broadcast_to(branch[LIVE_MAX : LIVE_MAX + 1], (rest, branch.shape[1])).astype(BF16)


def finish(branch, attended, w_out, normed):
    return pl.pallas_call(
        finish_kernel,
        in_specs=vmem(4),
        out_specs=pl.BlockSpec(memory_space=pltpu.VMEM),
        out_shape=jax.ShapeDtypeStruct((ANCH_DEV, branch.shape[1]), BF16),
        compiler_params=params(),
        name="finish",
    )(branch, attended, w_out, normed)


def pairs(move):
    found = []
    for z in range(4):
        for y in range(2):
            for core in range(2):
                for x in range(2):
                    to_z, to_y, to_core, to_x = move(z, y, core, x)
                    found.append((((z * 2 + y) * 2 + core) * 2 + x, ((to_z * 2 + to_y) * 2 + to_core) * 2 + to_x))
    return found


def send(array, move):
    return lax.ppermute(array, ALL, pairs(move))


def across_core(z, y, core, x):
    return z, y, 1 - core, x


def across_x(z, y, core, x):
    return z, y, core, 1 - x


def across_first(z, y, core, x):
    return (z, 1 - y, core, x) if core == 0 else (z, y, core, 1 - x)


def across_second(z, y, core, x):
    return (z, 1 - y, core, x) if core == 1 else (z, y, core, 1 - x)


def across_z(step):
    return lambda z, y, core, x: (z ^ step, y, core, x)


def halves(w):
    return w.reshape(2, w.shape[0] // 2, w.shape[1])


def block_plan(messages, node_anchor, anchor_count, norm_gain, w_query, w_key, w_value, w_out):
    channels = messages.shape[1]
    before, own, after = pool(messages, node_anchor)
    from_next = shift(before, -1)
    from_previous = shift(after, 1)
    mine = settle(anchor_count, own, from_next, from_previous)
    gain = norm_gain.reshape(2, 1, channels)
    wq, wk, wv, wo = halves(w_query), halves(w_key), halves(w_value), halves(w_out)
    slices = [mine] + [send(mine, across_z(step)) for step in (1, 2, 3)]
    states = []
    for index, rows in enumerate(slices):
        first = send(rows, across_first)
        second = send(join(rows, first, *states[: max(index - 1, 0)][-1:]), across_second)
        if index == 0:
            query, normed = make_queries(rows, first, second, gain, wq)
            swapped = send(query, across_core)
        states.append(attend(query, swapped, rows, first, second, gain, wk, wv, *states[-1:]))
    state = states[-1]
    other = send(state[:, QROWS - SENT :], across_core)
    attended = combine(state, other)
    attended_other = send(attended, across_x)
    branch = own_branch(attended, wo)
    return finish(branch, attended_other, wo, normed)


def shift(x, by):
    peers = lax.axis_size("ctx")
    return lax.ppermute(x, "ctx", [(i, (i + by) % peers) for i in range(peers)])


def pool_local(messages, node_anchor, center):
    partitions = lax.axis_size("ctx")
    owner_dev = node_anchor // ANCH_DEV
    offset = (owner_dev - center + 1 + partitions) % partitions
    local_slot = node_anchor % ANCH_DEV
    channel_count = messages.shape[1]
    tile_count = messages.shape[0] // 128
    group = math.gcd(tile_count, 4)
    steps_count = tile_count // group
    slot_blocks = local_slot.reshape(steps_count, group, 128)
    offset_blocks = offset.reshape(steps_count, group, 128)[:, :, 0]
    message_blocks = messages.reshape(steps_count, group, 128, channel_count)
    columns = jnp.arange(ANCH_DEV, dtype=jnp.int32)

    def add_block(running, pieces):
        slot_block, offset_block, message_block = pieces
        onehot = (slot_block[:, :, None] == columns[None, None, :]).astype(jnp.bfloat16)
        partial_value = jnp.einsum(
            "tnk,tnc->tkc", onehot, message_block, preferred_element_type=jnp.float32
        )
        for tile in range(group):
            where = offset_block[tile]
            current = lax.dynamic_index_in_dim(running, where, 0, keepdims=False)
            running = lax.dynamic_update_index_in_dim(
                running, current + partial_value[tile], where, 0
            )
        return (running, None)

    initial = jnp.zeros((3, ANCH_DEV, channel_count), jnp.float32)
    running, unused = lax.scan(add_block, initial, (slot_blocks, offset_blocks, message_blocks))
    return running


def make_fold(queries, shard_rows, scale):
    heads_local = queries.shape[1]

    def fold(carry, pieces, start_row):
        key_rows, value_rows, live_rows = pieces
        shards = live_rows.shape[0] // shard_rows
        key_blocks = key_rows.reshape(shards, shard_rows, heads_local, HD)
        value_blocks = value_rows.reshape(shards, shard_rows, heads_local, HD)
        live_blocks = live_rows.reshape(shards, shard_rows)

        def visit(state, block):
            highest, totals, accum = state
            key_block, value_block, live_block = block
            scores = (
                jnp.einsum("qhd,khd->hqk", queries, key_block, preferred_element_type=jnp.float32)
                * scale
            )
            alive = (live_block > 0)[None, None, :]
            scores = jnp.where(alive, scores, NEG)
            newest = jnp.maximum(highest, jnp.max(scores, axis=-1))
            weights = jnp.where(alive, jnp.exp(scores - newest[..., None]), 0.0)
            factor = jnp.exp(highest - newest)
            totals = totals * factor + jnp.sum(weights, axis=-1)
            mixed = jnp.einsum(
                "hqk,khd->hqd",
                weights.astype(jnp.bfloat16),
                value_block,
                preferred_element_type=jnp.float32,
            )
            accum = accum * factor[..., None] + mixed
            return ((newest, totals, accum), None)

        carry, unused = lax.scan(visit, carry, (key_blocks, value_blocks, live_blocks))
        return carry

    return fold


def general_plan(messages, node_anchor, anchor_count, norm_gain, w_query, w_key, w_value, w_out):
    center = lax.axis_index("ctx")
    pooled_terms = pool_local(messages, node_anchor, center)
    for_previous = pooled_terms[0]
    own_rows = pooled_terms[1]
    for_next = pooled_terms[2]
    from_next = shift(for_previous, -1)
    from_previous = shift(for_next, 1)
    sums = own_rows + from_next + from_previous
    pooled = sums.astype(jnp.bfloat16)
    whole = lax.all_gather(pooled, "head", axis=1, tiled=True).astype(jnp.float32)
    mean_square = jnp.mean(whole * whole, axis=1, keepdims=True)
    normed = (whole * lax.rsqrt(mean_square + EPS) * norm_gain).astype(jnp.bfloat16)
    channel_count = messages.shape[1]
    local_normed = lax.dynamic_slice_in_dim(
        normed, lax.axis_index("head") * channel_count, channel_count, 1
    )
    heads_local = w_query.shape[1] // HD
    queries = jnp.dot(normed, w_query, preferred_element_type=jnp.float32).astype(jnp.bfloat16)
    keys_local = jnp.dot(normed, w_key, preferred_element_type=jnp.float32).astype(jnp.bfloat16)
    values_local = jnp.dot(normed, w_value, preferred_element_type=jnp.float32).astype(jnp.bfloat16)
    queries = queries.reshape(ANCH_DEV, heads_local, HD)
    scale = HD ** (-0.5)
    initial = (
        jnp.full((heads_local, ANCH_DEV), NEG, jnp.float32),
        jnp.zeros((heads_local, ANCH_DEV), jnp.float32),
        jnp.zeros((heads_local, ANCH_DEV, HD), jnp.float32),
    )
    live_flags = (jnp.arange(ANCH_DEV, dtype=jnp.int32) < anchor_count[0]).astype(jnp.bfloat16)
    fold = make_fold(queries, ANCH_DEV, scale)
    highest, totals, accum = fold(
        initial,
        (
            lax.all_gather(keys_local, "ctx", axis=0, tiled=True),
            lax.all_gather(values_local, "ctx", axis=0, tiled=True),
            lax.all_gather(live_flags, "ctx", axis=0, tiled=True),
        ),
        jnp.int32(0),
    )
    attended = (
        (accum / totals[..., None])
        .transpose(1, 0, 2)
        .reshape(ANCH_DEV, heads_local * HD)
        .astype(jnp.bfloat16)
    )
    branch = jnp.dot(
        lax.all_gather(attended, "head", axis=1, tiled=True),
        w_out,
        preferred_element_type=jnp.float32,
    )
    return (local_normed.astype(jnp.float32) + branch).astype(jnp.bfloat16)


def solution(mesh):
    placed = (
        P("ctx", "head"),
        P("ctx"),
        P("ctx"),
        P(),
        P(None, "head"),
        P(None, "head"),
        P(None, "head"),
        P(None, "head"),
    )
    sizes = (mesh.shape["ctx"], mesh.shape["head"])
    plan = block_plan if sizes == (16, 2) else general_plan
    return jax.shard_map(plan, mesh=mesh, in_specs=placed, out_specs=P("ctx", "head"), check_vma=False)
```

```python
import functools
import math

import jax
import jax.numpy as jnp
from jax import lax
from jax.experimental import pallas as pl
from jax.experimental.pallas import tpu as pltpu
from jax.sharding import PartitionSpec as P

HD = 64
ANCH_DEV = 256
LIVE_MAX = 192
PAD = 16
QROWS = 2 * LIVE_MAX
SENT = 256
TILE = 128

EPS = 1e-06
NEG = -1e30
MARK = 2.0**100
MARKED = 2.0**90
RATE = HD**-0.5 * math.log2(math.e)

ALL = ("ctx", "head")
F32 = jnp.float32
BF16 = jnp.bfloat16


def params(mib=32):
    return pltpu.CompilerParams(vmem_limit_bytes=mib * 2**20)


def vmem(count):
    return [pl.BlockSpec(memory_space=pltpu.VMEM)] * count


def dot(a, b, contract=((1,), (0,))):
    return lax.dot_general(a, b, (contract, ((), ())), preferred_element_type=F32)


COPIES = 4
GROUP = 8


def pool_kernel(sides, anchors_hbm, messages_hbm, *refs):
    outs = refs[: len(sides)]
    anchors_smem, listed, anchors, messages, sems = refs[len(sides) :]
    partitions = lax.axis_size("ctx")
    center = lax.axis_index("ctx")
    tiles = anchors.shape[0]
    rows = tiles // COPIES * TILE
    loads = [
        pltpu.make_async_copy(anchors_hbm, anchors_smem, sems.at[COPIES]),
        pltpu.make_async_copy(anchors_hbm, anchors, sems.at[COPIES + 1]),
    ]
    for part in range(COPIES):
        at = pl.ds(part * rows, rows)
        loads.append(pltpu.make_async_copy(messages_hbm.at[at], messages.at[at], sems.at[part]))
    for load in loads:
        load.start()
    for out in outs:
        out[...] = jnp.zeros_like(out)
    slots = lax.broadcasted_iota(jnp.int32, (LIVE_MAX, TILE), 0)
    loads[0].wait()
    counts = [jnp.int32(0)] * len(sides)
    for tile in range(tiles):
        side = lax.rem(anchors_smem[tile, 0] // ANCH_DEV - center + 1 + partitions, partitions)
        for index, name in enumerate(sides):
            ahead = 1 if name == "own" else 2 * lax.rem(center, 2)
            which = 2 - ahead if name == "near" else ahead
            listed[index, counts[index]] = tile
            counts[index] = counts[index] + jnp.where(side == which, 1, 0)
    for load in loads[1:]:
        load.wait()
    for index, out in enumerate(outs):

        def add(group, unused, index=index, out=out):
            onehots, parts = [], []
            for at in range(GROUP):
                place = group * GROUP + at
                wanted = place < counts[index]
                tile = jnp.where(wanted, listed[index, jnp.minimum(place, tiles - 1)], 0)
                slot = jnp.where(wanted, anchors[pl.ds(tile, 1), :] % ANCH_DEV, -1)
                onehots.append(jnp.where(slots == slot, 1.0, 0.0).astype(BF16))
                parts.append(messages[pl.ds(pl.multiple_of(tile * TILE, TILE), TILE), :])
            out[...] += dot(jnp.concatenate(onehots, axis=1), jnp.concatenate(parts, axis=0))
            return unused

        lax.fori_loop(0, (counts[index] + GROUP - 1) // GROUP, add, 0)


def pool(messages, node_anchor, sides):
    nodes, channels = messages.shape
    tiles = nodes // TILE
    hbm = pl.BlockSpec(memory_space=pltpu.MemorySpace.HBM)
    return pl.pallas_call(
        functools.partial(pool_kernel, sides),
        in_specs=[hbm] * 2,
        out_specs=vmem(len(sides)),
        scratch_shapes=[
            pltpu.SMEM((tiles, TILE), jnp.int32),
            pltpu.SMEM((len(sides), tiles + 1), jnp.int32),
            pltpu.VMEM((tiles, TILE), jnp.int32),
            pltpu.VMEM((nodes, channels), BF16),
            pltpu.SemaphoreType.DMA((COPIES + 2,)),
        ],
        out_shape=[jax.ShapeDtypeStruct((LIVE_MAX, channels), F32)] * len(sides),
        compiler_params=params(60),
        cost_estimate=pl.CostEstimate(flops=10**9, bytes_accessed=5 * 10**6, transcendentals=0),
        name="pool",
    )(node_anchor.reshape(tiles, TILE), messages)


def after_kernel(a_ref, *rest):
    rest[-1][...] = a_ref[...]


def after(a, *others, cost=1):
    return pl.pallas_call(
        after_kernel,
        in_specs=vmem(1) + [pl.BlockSpec(memory_space=pl.ANY)] * len(others),
        out_specs=pl.BlockSpec(memory_space=pltpu.VMEM),
        out_shape=jax.ShapeDtypeStruct(a.shape, a.dtype),
        compiler_params=params(),
        cost_estimate=pl.CostEstimate(flops=cost, bytes_accessed=1, transcendentals=0),
        name="after",
    )(a, *others)


def settle(count, own, before, after):
    slot = lax.broadcasted_iota(jnp.int32, own.shape, 0)
    return jnp.where(slot < count, own + before + after, MARK).astype(BF16)


def join_kernel(a_ref, b_ref, out_ref):
    rows = a_ref.shape[0]
    out_ref[:rows, :] = a_ref[...]
    out_ref[rows:, :] = b_ref[...]


def join(a, b, cost=1):
    return pl.pallas_call(
        join_kernel,
        in_specs=vmem(2),
        out_specs=pl.BlockSpec(memory_space=pltpu.VMEM),
        out_shape=jax.ShapeDtypeStruct((a.shape[0] + b.shape[0], a.shape[1]), a.dtype),
        compiler_params=params(),
        cost_estimate=pl.CostEstimate(flops=cost, bytes_accessed=1, transcendentals=0),
        name="join",
    )(a, b)


def normalise(mine, other, gain_ref, x):
    channels = mine.shape[1]
    mine, other = mine.astype(F32), other.astype(F32)
    dead = mine[:, :1] > MARKED
    mine = jnp.where(dead, 0.0, mine)
    other = jnp.where(dead, 0.0, other)
    square = jnp.sum(mine * mine + other * other, axis=1, keepdims=True)
    inverse = lax.rsqrt(square * (1.0 / (2 * channels)) + EPS)
    mine = (mine * inverse * gain_ref[x]).astype(BF16)
    other = (other * inverse * gain_ref[1 - x]).astype(BF16)
    return mine, other, dead


def project(mine, other, w_ref, x):
    return (dot(mine, w_ref[x]) + dot(other, w_ref[1 - x])).astype(BF16)


def query_kernel(first_ref, second_ref, gain_ref, wq_ref, query_ref, normed_ref):
    core = lax.rem(lax.axis_index("ctx"), 2)
    x = lax.axis_index("head")
    other = jnp.where(core == 0, second_ref[:LIVE_MAX, :], first_ref[LIVE_MAX:, :])
    mine, other, unused = normalise(first_ref[:LIVE_MAX, :], other, gain_ref, x)
    query_ref[...] = project(mine, other, wq_ref, x)
    normed_ref[...] = mine


def make_queries(first, second, gain, wq):
    channels = first.shape[1]
    return pl.pallas_call(
        query_kernel,
        in_specs=vmem(4),
        out_specs=vmem(2),
        out_shape=[jax.ShapeDtypeStruct((LIVE_MAX, channels), BF16)] * 2,
        compiler_params=params(),
        cost_estimate=pl.CostEstimate(flops=1, bytes_accessed=1, transcendentals=0),
        name="queries",
    )(first, second, gain, wq)


def attend_kernel(first_call, *refs):
    if first_call:
        qm, qr, first_ref, second_ref, gain_ref, wk_ref, wv_ref, out_ref = refs
        state_ref = None
    else:
        qm, qr, first_ref, second_ref, gain_ref, wk_ref, wv_ref, state_ref, out_ref = refs
    core = lax.rem(lax.axis_index("ctx"), 2)
    x = lax.axis_index("head")
    channels = first_ref.shape[1]
    heads = channels // HD
    one, two = first_ref[LIVE_MAX:, :], second_ref[:LIVE_MAX, :]
    mine = jnp.concatenate([first_ref[:LIVE_MAX, :], jnp.where(core == 0, one, two)], axis=0)
    other = jnp.concatenate([jnp.where(core == 0, two, one), second_ref[LIVE_MAX:, :]], axis=0)
    mine, other, dead = normalise(mine, other, gain_ref, x)
    keys = project(mine, other, wk_ref, x)
    values = project(mine, other, wv_ref, x)
    shut = jnp.where(dead, NEG, 0.0).astype(BF16)

    live = jnp.sum(jnp.where(dead, 0.0, 1.0), axis=0, keepdims=True)
    live = jnp.broadcast_to(live, (1, SENT))
    value_sum = jnp.sum(values.astype(F32), axis=0, keepdims=True)
    extra = channels + 2 * heads
    for part in range(channels // SENT):
        at = value_sum[:, part * SENT : (part + 1) * SENT]
        row = slice(extra + part, extra + part + 1)
        out_ref[row, QROWS - SENT :] = at if first_call else at + state_ref[row, QROWS - SENT :]
    row = slice(extra + channels // SENT, extra + channels // SENT + 1)
    out_ref[row, QROWS - SENT :] = live if first_call else live + state_ref[row, QROWS - SENT :]
    values = values.T

    lane_k = lax.broadcasted_iota(jnp.int32, (keys.shape[0], 128), 1)
    lane_q = lax.broadcasted_iota(jnp.int32, (QROWS, 128), 1)

    def score(head):
        pair, side = head // 2, head % 2
        at = slice(pair * 128, (pair + 1) * 128)
        query = jnp.concatenate([qm[:, at], qr[128:, at], qr[:128, at]], axis=0)
        hot = jnp.where(lane_q == (1 - side) * HD, 1.0, 0.0).astype(BF16)
        q = jnp.where((lane_q // HD) == side, query, hot)
        k = jnp.where((lane_k // HD) == side, keys[:, at], shut)
        return dot(k, q, ((1,), (1,)))

    def weigh(head, scores):
        top = jnp.max(scores, axis=0, keepdims=True)
        at_top = slice(channels + head, channels + head + 1)
        at_total = slice(channels + heads + head, channels + heads + head + 1)
        fade = None
        if not first_call:
            old_top = state_ref[at_top, :]
            top = jnp.maximum(top, old_top)
            fade = jnp.exp2((old_top - top) * RATE)
        weights = jnp.exp2((scores - top) * RATE)
        total = jnp.sum(weights, axis=0, keepdims=True)
        if not first_call:
            total = total + state_ref[at_total, :] * fade
        out_ref[at_top, :] = top
        out_ref[at_total, :] = total
        return weights.astype(BF16), fade

    def mix(head, weights, fade):
        at = slice(head * HD, (head + 1) * HD)
        mixed = dot(values[at], weights)
        if not first_call:
            mixed = mixed + state_ref[at, :] * fade
        out_ref[at, :] = mixed

    scores = [score(head) for head in range(heads)]
    weights = [weigh(head, scores[head]) for head in range(heads)]
    for head in range(heads):
        mix(head, *weights[head])


def attend(qm, qr, first, second, gain, wk, wv, state=None):
    channels = first.shape[1]
    args = [qm, qr, first, second, gain, wk, wv] + ([] if state is None else [state])
    keys = 2 * LIVE_MAX
    return pl.pallas_call(
        functools.partial(attend_kernel, state is None),
        in_specs=vmem(len(args)),
        out_specs=pl.BlockSpec(memory_space=pltpu.VMEM),
        out_shape=jax.ShapeDtypeStruct((channels + 2 * (channels // HD) + 8, QROWS), F32),
        input_output_aliases={} if state is None else {len(args) - 1: 0},
        compiler_params=params(),
        cost_estimate=pl.CostEstimate(
            flops=1, bytes_accessed=1, transcendentals=0
        ),
        name="attend",
    )(*args)


def combine_kernel(mine_ref, other_ref, out_ref):
    channels = out_ref.shape[1]
    heads = channels // HD

    def theirs(at):
        middle = other_ref[at, :128]
        return jnp.concatenate([other_ref[at, 128:], middle[:, 64:], middle[:, :64]], axis=1)

    for head in range(heads):
        at_top = slice(channels + head, channels + head + 1)
        at_total = slice(channels + heads + head, channels + heads + head + 1)
        at = slice(head * HD, (head + 1) * HD)
        a, b = mine_ref[at_top, :SENT], theirs(at_top)
        top = jnp.maximum(a, b)
        a, b = jnp.exp2((a - top) * RATE), jnp.exp2((b - top) * RATE)
        total = mine_ref[at_total, :SENT] * a + theirs(at_total) * b
        mixed = (mine_ref[at, :SENT] * a + theirs(at) * b) / total
        out_ref[:LIVE_MAX, at] = mixed.T[:LIVE_MAX].astype(BF16)
    extra = channels + 2 * heads
    sums = mine_ref[extra : extra + 8, QROWS - SENT :] + other_ref[extra : extra + 8, :]
    parts = channels // SENT
    live = sums[parts : parts + 1, :]
    for part in range(parts):
        mean = (sums[part : part + 1, :] / live).astype(BF16)
        out_ref[LIVE_MAX:, part * SENT : (part + 1) * SENT] = jnp.broadcast_to(mean, (PAD, SENT))


def combine(mine, other):
    channels = other.shape[0] // (HD + 2) * HD
    return pl.pallas_call(
        combine_kernel,
        in_specs=vmem(2),
        out_specs=pl.BlockSpec(memory_space=pltpu.VMEM),
        out_shape=jax.ShapeDtypeStruct((LIVE_MAX + PAD, channels), BF16),
        compiler_params=params(),
        name="combine",
    )(mine, other)


def own_branch_kernel(attended_ref, w_ref, out_ref):
    out_ref[...] = dot(attended_ref[...], w_ref[lax.axis_index("head")])


def own_branch(attended, w_out):
    return pl.pallas_call(
        own_branch_kernel,
        in_specs=vmem(2),
        out_specs=pl.BlockSpec(memory_space=pltpu.VMEM),
        out_shape=jax.ShapeDtypeStruct((attended.shape[0], w_out.shape[2]), F32),
        compiler_params=params(),
        cost_estimate=pl.CostEstimate(flops=10**8, bytes_accessed=10**6, transcendentals=0),
        name="own_branch",
    )(attended, w_out)


def finish_kernel(branch_ref, attended_ref, w_ref, normed_ref, out_ref):
    branch = branch_ref[...] + dot(attended_ref[...], w_ref[1 - lax.axis_index("head")])
    out_ref[:LIVE_MAX, :] = (branch[:LIVE_MAX] + normed_ref[...].astype(F32)).astype(BF16)
    rest = out_ref.shape[0] - LIVE_MAX
    out_ref[LIVE_MAX:, :] = jnp.broadcast_to(branch[LIVE_MAX : LIVE_MAX + 1], (rest, branch.shape[1])).astype(BF16)


def finish(branch, attended, w_out, normed):
    return pl.pallas_call(
        finish_kernel,
        in_specs=vmem(4),
        out_specs=pl.BlockSpec(memory_space=pltpu.VMEM),
        out_shape=jax.ShapeDtypeStruct((ANCH_DEV, branch.shape[1]), BF16),
        compiler_params=params(),
        name="finish",
    )(branch, attended, w_out, normed)


def pairs(move):
    found = []
    for z in range(4):
        for y in range(2):
            for core in range(2):
                for x in range(2):
                    to_z, to_y, to_core, to_x = move(z, y, core, x)
                    found.append((((z * 2 + y) * 2 + core) * 2 + x, ((to_z * 2 + to_y) * 2 + to_core) * 2 + to_x))
    return found


def send(array, move):
    return lax.ppermute(array, ALL, pairs(move))


def across_core(z, y, core, x):
    return z, y, 1 - core, x


def across_x(z, y, core, x):
    return z, y, core, 1 - x


def across_first(z, y, core, x):
    return (z, 1 - y, core, x) if core == 0 else (z, y, core, 1 - x)


def across_second(z, y, core, x):
    return (z, 1 - y, core, x) if core == 1 else (z, y, core, 1 - x)


def across_z(step):
    return lambda z, y, core, x: (z ^ step, y, core, x)


def halves(w):
    return w.reshape(2, w.shape[0] // 2, w.shape[1])


def block_plan(messages, node_anchor, anchor_count, norm_gain, w_query, w_key, w_value, w_out):
    channels = messages.shape[1]
    far, near = pool(messages, node_anchor, ("far", "near"))
    (own,) = pool(messages, node_anchor, ("own",))
    from_far = lax.ppermute(far, "ctx", [(i, (i + (1 if i % 2 else 15)) % 16) for i in range(16)])
    from_near = send(near, across_core)
    mine = settle(anchor_count, own, from_far, from_near)
    gain = norm_gain.reshape(2, 1, channels)
    wq, wk, wv, wo = halves(w_query), halves(w_key), halves(w_value), halves(w_out)
    far_rows = [send(mine, across_z(step)) for step in (2, 3)]
    first = join(mine, send(mine, across_first))
    second = send(first, across_second)
    query, normed = make_queries(first, second, gain, wq)
    swapped = send(query, across_core)
    beside = [send(first, across_z(1)), send(second, across_z(1))]
    state = attend(query, swapped, first, second, gain, wk, wv)
    states = [state, attend(query, swapped, *beside, gain, wk, wv, state)]
    plane = first
    for index, rows in enumerate(far_rows):
        rows = after(rows, plane, cost=2*10**10)
        first = join(rows, send(rows, across_first), cost=10**10)
        second = send(first, across_second)
        states.append(attend(query, swapped, first, second, gain, wk, wv, states[-1]))
    state = states[-1]
    other = send(state[:, QROWS - SENT :], across_core)
    attended = combine(state, other)
    attended_other = send(attended, across_x)
    branch = own_branch(attended, wo)
    return finish(branch, attended_other, wo, normed)


def shift(x, by):
    peers = lax.axis_size("ctx")
    return lax.ppermute(x, "ctx", [(i, (i + by) % peers) for i in range(peers)])


def pool_local(messages, node_anchor, center):
    partitions = lax.axis_size("ctx")
    owner_dev = node_anchor // ANCH_DEV
    offset = (owner_dev - center + 1 + partitions) % partitions
    local_slot = node_anchor % ANCH_DEV
    channel_count = messages.shape[1]
    tile_count = messages.shape[0] // 128
    group = math.gcd(tile_count, 4)
    steps_count = tile_count // group
    slot_blocks = local_slot.reshape(steps_count, group, 128)
    offset_blocks = offset.reshape(steps_count, group, 128)[:, :, 0]
    message_blocks = messages.reshape(steps_count, group, 128, channel_count)
    columns = jnp.arange(ANCH_DEV, dtype=jnp.int32)

    def add_block(running, pieces):
        slot_block, offset_block, message_block = pieces
        onehot = (slot_block[:, :, None] == columns[None, None, :]).astype(jnp.bfloat16)
        partial_value = jnp.einsum(
            "tnk,tnc->tkc", onehot, message_block, preferred_element_type=jnp.float32
        )
        for tile in range(group):
            where = offset_block[tile]
            current = lax.dynamic_index_in_dim(running, where, 0, keepdims=False)
            running = lax.dynamic_update_index_in_dim(
                running, current + partial_value[tile], where, 0
            )
        return (running, None)

    initial = jnp.zeros((3, ANCH_DEV, channel_count), jnp.float32)
    running, unused = lax.scan(add_block, initial, (slot_blocks, offset_blocks, message_blocks))
    return running


def make_fold(queries, shard_rows, scale):
    heads_local = queries.shape[1]

    def fold(carry, pieces, start_row):
        key_rows, value_rows, live_rows = pieces
        shards = live_rows.shape[0] // shard_rows
        key_blocks = key_rows.reshape(shards, shard_rows, heads_local, HD)
        value_blocks = value_rows.reshape(shards, shard_rows, heads_local, HD)
        live_blocks = live_rows.reshape(shards, shard_rows)

        def visit(state, block):
            highest, totals, accum = state
            key_block, value_block, live_block = block
            scores = (
                jnp.einsum("qhd,khd->hqk", queries, key_block, preferred_element_type=jnp.float32)
                * scale
            )
            alive = (live_block > 0)[None, None, :]
            scores = jnp.where(alive, scores, NEG)
            newest = jnp.maximum(highest, jnp.max(scores, axis=-1))
            weights = jnp.where(alive, jnp.exp(scores - newest[..., None]), 0.0)
            factor = jnp.exp(highest - newest)
            totals = totals * factor + jnp.sum(weights, axis=-1)
            mixed = jnp.einsum(
                "hqk,khd->hqd",
                weights.astype(jnp.bfloat16),
                value_block,
                preferred_element_type=jnp.float32,
            )
            accum = accum * factor[..., None] + mixed
            return ((newest, totals, accum), None)

        carry, unused = lax.scan(visit, carry, (key_blocks, value_blocks, live_blocks))
        return carry

    return fold


def general_plan(messages, node_anchor, anchor_count, norm_gain, w_query, w_key, w_value, w_out):
    center = lax.axis_index("ctx")
    pooled_terms = pool_local(messages, node_anchor, center)
    for_previous = pooled_terms[0]
    own_rows = pooled_terms[1]
    for_next = pooled_terms[2]
    from_next = shift(for_previous, -1)
    from_previous = shift(for_next, 1)
    sums = own_rows + from_next + from_previous
    pooled = sums.astype(jnp.bfloat16)
    whole = lax.all_gather(pooled, "head", axis=1, tiled=True).astype(jnp.float32)
    mean_square = jnp.mean(whole * whole, axis=1, keepdims=True)
    normed = (whole * lax.rsqrt(mean_square + EPS) * norm_gain).astype(jnp.bfloat16)
    channel_count = messages.shape[1]
    local_normed = lax.dynamic_slice_in_dim(
        normed, lax.axis_index("head") * channel_count, channel_count, 1
    )
    heads_local = w_query.shape[1] // HD
    queries = jnp.dot(normed, w_query, preferred_element_type=jnp.float32).astype(jnp.bfloat16)
    keys_local = jnp.dot(normed, w_key, preferred_element_type=jnp.float32).astype(jnp.bfloat16)
    values_local = jnp.dot(normed, w_value, preferred_element_type=jnp.float32).astype(jnp.bfloat16)
    queries = queries.reshape(ANCH_DEV, heads_local, HD)
    scale = HD ** (-0.5)
    initial = (
        jnp.full((heads_local, ANCH_DEV), NEG, jnp.float32),
        jnp.zeros((heads_local, ANCH_DEV), jnp.float32),
        jnp.zeros((heads_local, ANCH_DEV, HD), jnp.float32),
    )
    live_flags = (jnp.arange(ANCH_DEV, dtype=jnp.int32) < anchor_count[0]).astype(jnp.bfloat16)
    fold = make_fold(queries, ANCH_DEV, scale)
    highest, totals, accum = fold(
        initial,
        (
            lax.all_gather(keys_local, "ctx", axis=0, tiled=True),
            lax.all_gather(values_local, "ctx", axis=0, tiled=True),
            lax.all_gather(live_flags, "ctx", axis=0, tiled=True),
        ),
        jnp.int32(0),
    )
    attended = (
        (accum / totals[..., None])
        .transpose(1, 0, 2)
        .reshape(ANCH_DEV, heads_local * HD)
        .astype(jnp.bfloat16)
    )
    branch = jnp.dot(
        lax.all_gather(attended, "head", axis=1, tiled=True),
        w_out,
        preferred_element_type=jnp.float32,
    )
    return (local_normed.astype(jnp.float32) + branch).astype(jnp.bfloat16)


def solution(mesh):
    placed = (
        P("ctx", "head"),
        P("ctx"),
        P("ctx"),
        P(),
        P(None, "head"),
        P(None, "head"),
        P(None, "head"),
        P(None, "head"),
    )
    sizes = (mesh.shape["ctx"], mesh.shape["head"])
    plan = block_plan if sizes == (16, 2) else general_plan
    return jax.shard_map(plan, mesh=mesh, in_specs=placed, out_specs=P("ctx", "head"), check_vma=False)
```

```python
import functools
import math

import jax
import jax.numpy as jnp
from jax import lax
from jax.experimental import pallas as pl
from jax.experimental.pallas import tpu as pltpu
from jax.sharding import PartitionSpec as P

HD = 64
ANCH_DEV = 256
LIVE_MAX = 192
PAD = 16
QROWS = 2 * LIVE_MAX
SENT = 256
TILE = 128

EPS = 1e-06
NEG = -1e30
MARK = 2.0**50
MARKED = 2.0**40
RATE = HD**-0.5 * math.log2(math.e)

ALL = ("ctx", "head")
F32 = jnp.float32
BF16 = jnp.bfloat16


def params(mib=32):
    return pltpu.CompilerParams(vmem_limit_bytes=mib * 2**20)


def vmem(count):
    return [pl.BlockSpec(memory_space=pltpu.VMEM)] * count


def dot(a, b, contract=((1,), (0,))):
    return lax.dot_general(a, b, (contract, ((), ())), preferred_element_type=F32)


COPIES = 4
GROUP = 8


def pool_kernel(sides, anchors_hbm, messages_hbm, *refs):
    outs = refs[: len(sides)]
    anchors_smem, listed, anchors, messages, sems = refs[len(sides) :]
    partitions = lax.axis_size("ctx")
    center = lax.axis_index("ctx")
    tiles = anchors.shape[0]
    rows = tiles // COPIES * TILE
    loads = [
        pltpu.make_async_copy(anchors_hbm, anchors_smem, sems.at[COPIES]),
        pltpu.make_async_copy(anchors_hbm, anchors, sems.at[COPIES + 1]),
    ]
    for part in range(COPIES):
        at = pl.ds(part * rows, rows)
        loads.append(pltpu.make_async_copy(messages_hbm.at[at], messages.at[at], sems.at[part]))
    for load in loads:
        load.start()
    for out in outs:
        out[...] = jnp.zeros_like(out)
    slots = lax.broadcasted_iota(jnp.int32, (LIVE_MAX, TILE), 0)
    loads[0].wait()
    counts = [jnp.int32(0)] * len(sides)
    for tile in range(tiles):
        side = lax.rem(anchors_smem[tile, 0] // ANCH_DEV - center + 1 + partitions, partitions)
        for index, name in enumerate(sides):
            ahead = 1 if name == "own" else 2 * lax.rem(center, 2)
            which = 2 - ahead if name == "near" else ahead
            listed[index, counts[index]] = tile
            counts[index] = counts[index] + jnp.where(side == which, 1, 0)
    for load in loads[1:]:
        load.wait()
    for index, out in enumerate(outs):

        def add(group, unused, index=index, out=out):
            onehots, parts = [], []
            for at in range(GROUP):
                place = group * GROUP + at
                wanted = place < counts[index]
                tile = jnp.where(wanted, listed[index, jnp.minimum(place, tiles - 1)], 0)
                slot = jnp.where(wanted, anchors[pl.ds(tile, 1), :] % ANCH_DEV, -1)
                onehots.append(jnp.where(slots == slot, 1.0, 0.0).astype(BF16))
                parts.append(messages[pl.ds(pl.multiple_of(tile * TILE, TILE), TILE), :])
            out[...] += dot(jnp.concatenate(onehots, axis=1), jnp.concatenate(parts, axis=0))
            return unused

        lax.fori_loop(0, (counts[index] + GROUP - 1) // GROUP, add, 0)


def pool(messages, node_anchor, sides):
    nodes, channels = messages.shape
    tiles = nodes // TILE
    hbm = pl.BlockSpec(memory_space=pltpu.MemorySpace.HBM)
    return pl.pallas_call(
        functools.partial(pool_kernel, sides),
        in_specs=[hbm] * 2,
        out_specs=vmem(len(sides)),
        scratch_shapes=[
            pltpu.SMEM((tiles, TILE), jnp.int32),
            pltpu.SMEM((len(sides), tiles + 1), jnp.int32),
            pltpu.VMEM((tiles, TILE), jnp.int32),
            pltpu.VMEM((nodes, channels), BF16),
            pltpu.SemaphoreType.DMA((COPIES + 2,)),
        ],
        out_shape=[jax.ShapeDtypeStruct((LIVE_MAX, channels), F32)] * len(sides),
        compiler_params=params(56),
        cost_estimate=pl.CostEstimate(flops=10**9, bytes_accessed=5 * 10**6, transcendentals=0),
        name="pool",
    )(node_anchor.reshape(tiles, TILE), messages)


def after_kernel(a_ref, *rest):
    rest[-1][...] = a_ref[...]


def after(a, *others, cost=1):
    return pl.pallas_call(
        after_kernel,
        in_specs=vmem(1) + [pl.BlockSpec(memory_space=pl.ANY)] * len(others),
        out_specs=pl.BlockSpec(memory_space=pltpu.VMEM),
        out_shape=jax.ShapeDtypeStruct(a.shape, a.dtype),
        compiler_params=params(),
        cost_estimate=pl.CostEstimate(flops=cost, bytes_accessed=1, transcendentals=0),
        name="after",
    )(a, *others)


def settle_kernel(count_ref, own_ref, far_ref, near_ref, out_ref):
    total = own_ref[...] + far_ref[...] + near_ref[...]
    slot = lax.broadcasted_iota(jnp.int32, total.shape, 0)
    out_ref[...] = jnp.where(slot < count_ref[0], total, MARK).astype(BF16)


def settle(count, own, far, near):
    return pl.pallas_call(
        settle_kernel,
        in_specs=[pl.BlockSpec(memory_space=pltpu.SMEM)] + vmem(3),
        out_specs=pl.BlockSpec(memory_space=pltpu.VMEM),
        out_shape=jax.ShapeDtypeStruct(own.shape, BF16),
        compiler_params=params(),
        name="settle",
    )(count, own, far, near)


def join_kernel(a_ref, b_ref, *rest):
    out_ref = rest[-1]
    rows = a_ref.shape[0]
    out_ref[:rows, :] = a_ref[...]
    out_ref[rows:, :] = b_ref[...]


def join(a, b, *others, cost=1):
    return pl.pallas_call(
        join_kernel,
        in_specs=vmem(2) + [pl.BlockSpec(memory_space=pl.ANY)] * len(others),
        out_specs=pl.BlockSpec(memory_space=pltpu.VMEM),
        out_shape=jax.ShapeDtypeStruct((a.shape[0] + b.shape[0], a.shape[1]), a.dtype),
        compiler_params=params(),
        cost_estimate=pl.CostEstimate(flops=cost, bytes_accessed=1, transcendentals=0),
        name="join",
    )(a, b, *others)


def normalise(mine, other, gain_ref, x):
    channels = mine.shape[1]
    mine, other = mine.astype(F32), other.astype(F32)
    dead = mine[:, :1] > MARKED
    square = jnp.sum(mine * mine + other * other, axis=1, keepdims=True)
    inverse = jnp.where(dead, 0.0, lax.rsqrt(square * (1.0 / (2 * channels)) + EPS))
    mine = (mine * inverse * gain_ref[x]).astype(BF16)
    other = (other * inverse * gain_ref[1 - x]).astype(BF16)
    return mine, other, dead


def project(mine, other, w_ref, x):
    return (dot(mine, w_ref[x]) + dot(other, w_ref[1 - x])).astype(BF16)


def query_kernel(first_ref, second_ref, gain_ref, wq_ref, query_ref, normed_ref):
    core = lax.rem(lax.axis_index("ctx"), 2)
    x = lax.axis_index("head")
    other = jnp.where(core == 0, second_ref[:LIVE_MAX, :], first_ref[LIVE_MAX:, :])
    mine, other, unused = normalise(first_ref[:LIVE_MAX, :], other, gain_ref, x)
    query_ref[...] = project(mine, other, wq_ref, x)
    normed_ref[...] = mine


def make_queries(first, second, gain, wq):
    channels = first.shape[1]
    return pl.pallas_call(
        query_kernel,
        in_specs=vmem(4),
        out_specs=vmem(2),
        out_shape=[jax.ShapeDtypeStruct((LIVE_MAX, channels), BF16)] * 2,
        compiler_params=params(),
        cost_estimate=pl.CostEstimate(flops=10**10, bytes_accessed=1, transcendentals=0),
        name="queries",
    )(first, second, gain, wq)


def attend_kernel(first_call, *refs):
    if first_call:
        qm, qr, first_ref, second_ref, gain_ref, wk_ref, wv_ref, out_ref = refs
        state_ref = None
    else:
        qm, qr, first_ref, second_ref, gain_ref, wk_ref, wv_ref, state_ref, out_ref = refs
    core = lax.rem(lax.axis_index("ctx"), 2)
    x = lax.axis_index("head")
    channels = first_ref.shape[1]
    heads = channels // HD
    one, two = first_ref[LIVE_MAX:, :], second_ref[:LIVE_MAX, :]
    mine = jnp.concatenate([first_ref[:LIVE_MAX, :], jnp.where(core == 0, one, two)], axis=0)
    other = jnp.concatenate([jnp.where(core == 0, two, one), second_ref[LIVE_MAX:, :]], axis=0)
    mine, other, dead = normalise(mine, other, gain_ref, x)
    keys = project(mine, other, wk_ref, x)
    values = project(mine, other, wv_ref, x)
    shut = jnp.where(dead, NEG, 0.0).astype(BF16)

    live = jnp.sum(jnp.where(dead, 0.0, 1.0), axis=0, keepdims=True)
    live = jnp.broadcast_to(live, (1, SENT))
    value_sum = jnp.sum(values.astype(F32), axis=0, keepdims=True)
    extra = channels + 2 * heads
    for part in range(channels // SENT):
        at = value_sum[:, part * SENT : (part + 1) * SENT]
        row = slice(extra + part, extra + part + 1)
        out_ref[row, QROWS - SENT :] = at if first_call else at + state_ref[row, QROWS - SENT :]
    row = slice(extra + channels // SENT, extra + channels // SENT + 1)
    out_ref[row, QROWS - SENT :] = live if first_call else live + state_ref[row, QROWS - SENT :]
    values = values.T

    lane_k = lax.broadcasted_iota(jnp.int32, (keys.shape[0], 128), 1)
    lane_q = lax.broadcasted_iota(jnp.int32, (QROWS, 128), 1)

    def score(head):
        pair, side = head // 2, head % 2
        at = slice(pair * 128, (pair + 1) * 128)
        query = jnp.concatenate([qm[:, at], qr[128:, at], qr[:128, at]], axis=0)
        hot = jnp.where(lane_q == (1 - side) * HD, 1.0, 0.0).astype(BF16)
        q = jnp.where((lane_q // HD) == side, query, hot)
        k = jnp.where((lane_k // HD) == side, keys[:, at], shut)
        return dot(k, q, ((1,), (1,)))

    def weigh(head, scores):
        top = jnp.max(scores, axis=0, keepdims=True)
        at_top = slice(channels + head, channels + head + 1)
        at_total = slice(channels + heads + head, channels + heads + head + 1)
        fade = None
        if not first_call:
            old_top = state_ref[at_top, :]
            top = jnp.maximum(top, old_top)
            fade = jnp.exp2((old_top - top) * RATE)
        weights = jnp.exp2((scores - top) * RATE)
        total = jnp.sum(weights, axis=0, keepdims=True)
        if not first_call:
            total = total + state_ref[at_total, :] * fade
        out_ref[at_top, :] = top
        out_ref[at_total, :] = total
        return weights.astype(BF16), fade

    def mix(head, weights, fade):
        at = slice(head * HD, (head + 1) * HD)
        mixed = dot(values[at], weights)
        if not first_call:
            mixed = mixed + state_ref[at, :] * fade
        out_ref[at, :] = mixed

    scores = [score(head) for head in range(heads)]
    weights = [weigh(head, scores[head]) for head in range(heads)]
    for head in range(heads):
        mix(head, *weights[head])


def attend(qm, qr, first, second, gain, wk, wv, state=None):
    channels = first.shape[1]
    args = [qm, qr, first, second, gain, wk, wv] + ([] if state is None else [state])
    keys = 2 * LIVE_MAX
    return pl.pallas_call(
        functools.partial(attend_kernel, state is None),
        in_specs=vmem(len(args)),
        out_specs=pl.BlockSpec(memory_space=pltpu.VMEM),
        out_shape=jax.ShapeDtypeStruct((channels + 2 * (channels // HD) + 8, QROWS), F32),
        input_output_aliases={} if state is None else {len(args) - 1: 0},
        compiler_params=params(),
        cost_estimate=pl.CostEstimate(
            flops=2*10**9, bytes_accessed=1, transcendentals=0
        ),
        name="attend",
    )(*args)


def combine_kernel(mine_ref, other_ref, out_ref):
    channels = out_ref.shape[1]
    heads = channels // HD

    def theirs(at):
        middle = other_ref[at, :128]
        return jnp.concatenate([other_ref[at, 128:], middle[:, 64:], middle[:, :64]], axis=1)

    for head in range(heads):
        at_top = slice(channels + head, channels + head + 1)
        at_total = slice(channels + heads + head, channels + heads + head + 1)
        at = slice(head * HD, (head + 1) * HD)
        a, b = mine_ref[at_top, :SENT], theirs(at_top)
        top = jnp.maximum(a, b)
        a, b = jnp.exp2((a - top) * RATE), jnp.exp2((b - top) * RATE)
        total = mine_ref[at_total, :SENT] * a + theirs(at_total) * b
        mixed = (mine_ref[at, :SENT] * a + theirs(at) * b) / total
        out_ref[:LIVE_MAX, at] = mixed.T[:LIVE_MAX].astype(BF16)
    extra = channels + 2 * heads
    sums = mine_ref[extra : extra + 8, QROWS - SENT :] + other_ref[extra : extra + 8, :]
    parts = channels // SENT
    live = sums[parts : parts + 1, :]
    for part in range(parts):
        mean = (sums[part : part + 1, :] / live).astype(BF16)
        out_ref[LIVE_MAX:, part * SENT : (part + 1) * SENT] = jnp.broadcast_to(mean, (PAD, SENT))


def combine(mine, other):
    channels = other.shape[0] // (HD + 2) * HD
    return pl.pallas_call(
        combine_kernel,
        in_specs=vmem(2),
        out_specs=pl.BlockSpec(memory_space=pltpu.VMEM),
        out_shape=jax.ShapeDtypeStruct((LIVE_MAX + PAD, channels), BF16),
        compiler_params=params(),
        name="combine",
    )(mine, other)


def own_branch_kernel(attended_ref, w_ref, out_ref):
    out_ref[...] = dot(attended_ref[...], w_ref[lax.axis_index("head")])


def own_branch(attended, w_out):
    return pl.pallas_call(
        own_branch_kernel,
        in_specs=vmem(2),
        out_specs=pl.BlockSpec(memory_space=pltpu.VMEM),
        out_shape=jax.ShapeDtypeStruct((attended.shape[0], w_out.shape[2]), F32),
        compiler_params=params(),
        cost_estimate=pl.CostEstimate(flops=10**8, bytes_accessed=10**6, transcendentals=0),
        name="own_branch",
    )(attended, w_out)


def finish_kernel(branch_ref, attended_ref, w_ref, normed_ref, out_ref):
    branch = branch_ref[...] + dot(attended_ref[...], w_ref[1 - lax.axis_index("head")])
    out_ref[:LIVE_MAX, :] = (branch[:LIVE_MAX] + normed_ref[...].astype(F32)).astype(BF16)
    rest = out_ref.shape[0] - LIVE_MAX
    out_ref[LIVE_MAX:, :] = jnp.broadcast_to(branch[LIVE_MAX : LIVE_MAX + 1], (rest, branch.shape[1])).astype(BF16)


def finish(branch, attended, w_out, normed):
    return pl.pallas_call(
        finish_kernel,
        in_specs=vmem(4),
        out_specs=pl.BlockSpec(memory_space=pltpu.VMEM),
        out_shape=jax.ShapeDtypeStruct((ANCH_DEV, branch.shape[1]), BF16),
        compiler_params=params(),
        name="finish",
    )(branch, attended, w_out, normed)


def pairs(move):
    found = []
    for z in range(4):
        for y in range(2):
            for core in range(2):
                for x in range(2):
                    to_z, to_y, to_core, to_x = move(z, y, core, x)
                    found.append((((z * 2 + y) * 2 + core) * 2 + x, ((to_z * 2 + to_y) * 2 + to_core) * 2 + to_x))
    return found


def send(array, move):
    return lax.ppermute(array, ALL, pairs(move))


def across_core(z, y, core, x):
    return z, y, 1 - core, x


def across_x(z, y, core, x):
    return z, y, core, 1 - x


def across_first(z, y, core, x):
    return (z, 1 - y, core, x) if core == 0 else (z, y, core, 1 - x)


def across_second(z, y, core, x):
    return (z, 1 - y, core, x) if core == 1 else (z, y, core, 1 - x)


def across_z(step):
    return lambda z, y, core, x: (z ^ step, y, core, x)


def halves(w):
    return w.reshape(2, w.shape[0] // 2, w.shape[1])


def block_plan(messages, node_anchor, anchor_count, norm_gain, w_query, w_key, w_value, w_out):
    channels = messages.shape[1]
    far, near = pool(messages, node_anchor, ("far", "near"))
    (own,) = pool(messages, node_anchor, ("own",))
    from_far = lax.ppermute(far, "ctx", [(i, (i + (1 if i % 2 else 15)) % 16) for i in range(16)])
    from_near = send(near, across_core)
    mine = settle(anchor_count, own, from_far, from_near)
    gain = norm_gain.reshape(2, 1, channels)
    wq, wk, wv, wo = halves(w_query), halves(w_key), halves(w_value), halves(w_out)
    far_rows = [send(mine, across_z(step)) for step in (2, 3)]
    first = join(mine, send(mine, across_first))
    second = send(first, across_second)
    query, normed = make_queries(first, second, gain, wq)
    swapped = send(query, across_core)
    beside = [send(first, across_z(1)), send(second, across_z(1))]
    state = attend(query, swapped, first, second, gain, wk, wv)
    states = [state, attend(query, swapped, *beside, gain, wk, wv, state)]
    gates = (first, query)
    for index, rows in enumerate(far_rows):
        rows = after(rows, gates[index], cost=(2 * 10**10, 5 * 10**9)[index])
        first = join(rows, send(rows, across_first), *([] if index else [state]), cost=3 * 10**10)
        second = send(first, across_second)
        states.append(attend(query, swapped, first, second, gain, wk, wv, states[-1]))
    state = states[-1]
    other = send(state[:, QROWS - SENT :], across_core)
    attended = combine(state, other)
    attended_other = send(attended, across_x)
    branch = own_branch(attended, wo)
    return finish(branch, attended_other, wo, normed)


def shift(x, by):
    peers = lax.axis_size("ctx")
    return lax.ppermute(x, "ctx", [(i, (i + by) % peers) for i in range(peers)])


def pool_local(messages, node_anchor, center):
    partitions = lax.axis_size("ctx")
    owner_dev = node_anchor // ANCH_DEV
    offset = (owner_dev - center + 1 + partitions) % partitions
    local_slot = node_anchor % ANCH_DEV
    channel_count = messages.shape[1]
    tile_count = messages.shape[0] // 128
    group = math.gcd(tile_count, 4)
    steps_count = tile_count // group
    slot_blocks = local_slot.reshape(steps_count, group, 128)
    offset_blocks = offset.reshape(steps_count, group, 128)[:, :, 0]
    message_blocks = messages.reshape(steps_count, group, 128, channel_count)
    columns = jnp.arange(ANCH_DEV, dtype=jnp.int32)

    def add_block(running, pieces):
        slot_block, offset_block, message_block = pieces
        onehot = (slot_block[:, :, None] == columns[None, None, :]).astype(jnp.bfloat16)
        partial_value = jnp.einsum(
            "tnk,tnc->tkc", onehot, message_block, preferred_element_type=jnp.float32
        )
        for tile in range(group):
            where = offset_block[tile]
            current = lax.dynamic_index_in_dim(running, where, 0, keepdims=False)
            running = lax.dynamic_update_index_in_dim(
                running, current + partial_value[tile], where, 0
            )
        return (running, None)

    initial = jnp.zeros((3, ANCH_DEV, channel_count), jnp.float32)
    running, unused = lax.scan(add_block, initial, (slot_blocks, offset_blocks, message_blocks))
    return running


def make_fold(queries, shard_rows, scale):
    heads_local = queries.shape[1]

    def fold(carry, pieces, start_row):
        key_rows, value_rows, live_rows = pieces
        shards = live_rows.shape[0] // shard_rows
        key_blocks = key_rows.reshape(shards, shard_rows, heads_local, HD)
        value_blocks = value_rows.reshape(shards, shard_rows, heads_local, HD)
        live_blocks = live_rows.reshape(shards, shard_rows)

        def visit(state, block):
            highest, totals, accum = state
            key_block, value_block, live_block = block
            scores = (
                jnp.einsum("qhd,khd->hqk", queries, key_block, preferred_element_type=jnp.float32)
                * scale
            )
            alive = (live_block > 0)[None, None, :]
            scores = jnp.where(alive, scores, NEG)
            newest = jnp.maximum(highest, jnp.max(scores, axis=-1))
            weights = jnp.where(alive, jnp.exp(scores - newest[..., None]), 0.0)
            factor = jnp.exp(highest - newest)
            totals = totals * factor + jnp.sum(weights, axis=-1)
            mixed = jnp.einsum(
                "hqk,khd->hqd",
                weights.astype(jnp.bfloat16),
                value_block,
                preferred_element_type=jnp.float32,
            )
            accum = accum * factor[..., None] + mixed
            return ((newest, totals, accum), None)

        carry, unused = lax.scan(visit, carry, (key_blocks, value_blocks, live_blocks))
        return carry

    return fold


def general_plan(messages, node_anchor, anchor_count, norm_gain, w_query, w_key, w_value, w_out):
    center = lax.axis_index("ctx")
    pooled_terms = pool_local(messages, node_anchor, center)
    for_previous = pooled_terms[0]
    own_rows = pooled_terms[1]
    for_next = pooled_terms[2]
    from_next = shift(for_previous, -1)
    from_previous = shift(for_next, 1)
    sums = own_rows + from_next + from_previous
    pooled = sums.astype(jnp.bfloat16)
    whole = lax.all_gather(pooled, "head", axis=1, tiled=True).astype(jnp.float32)
    mean_square = jnp.mean(whole * whole, axis=1, keepdims=True)
    normed = (whole * lax.rsqrt(mean_square + EPS) * norm_gain).astype(jnp.bfloat16)
    channel_count = messages.shape[1]
    local_normed = lax.dynamic_slice_in_dim(
        normed, lax.axis_index("head") * channel_count, channel_count, 1
    )
    heads_local = w_query.shape[1] // HD
    queries = jnp.dot(normed, w_query, preferred_element_type=jnp.float32).astype(jnp.bfloat16)
    keys_local = jnp.dot(normed, w_key, preferred_element_type=jnp.float32).astype(jnp.bfloat16)
    values_local = jnp.dot(normed, w_value, preferred_element_type=jnp.float32).astype(jnp.bfloat16)
    queries = queries.reshape(ANCH_DEV, heads_local, HD)
    scale = HD ** (-0.5)
    initial = (
        jnp.full((heads_local, ANCH_DEV), NEG, jnp.float32),
        jnp.zeros((heads_local, ANCH_DEV), jnp.float32),
        jnp.zeros((heads_local, ANCH_DEV, HD), jnp.float32),
    )
    live_flags = (jnp.arange(ANCH_DEV, dtype=jnp.int32) < anchor_count[0]).astype(jnp.bfloat16)
    fold = make_fold(queries, ANCH_DEV, scale)
    highest, totals, accum = fold(
        initial,
        (
            lax.all_gather(keys_local, "ctx", axis=0, tiled=True),
            lax.all_gather(values_local, "ctx", axis=0, tiled=True),
            lax.all_gather(live_flags, "ctx", axis=0, tiled=True),
        ),
        jnp.int32(0),
    )
    attended = (
        (accum / totals[..., None])
        .transpose(1, 0, 2)
        .reshape(ANCH_DEV, heads_local * HD)
        .astype(jnp.bfloat16)
    )
    branch = jnp.dot(
        lax.all_gather(attended, "head", axis=1, tiled=True),
        w_out,
        preferred_element_type=jnp.float32,
    )
    return (local_normed.astype(jnp.float32) + branch).astype(jnp.bfloat16)


def solution(mesh):
    placed = (
        P("ctx", "head"),
        P("ctx"),
        P("ctx"),
        P(),
        P(None, "head"),
        P(None, "head"),
        P(None, "head"),
        P(None, "head"),
    )
    sizes = (mesh.shape["ctx"], mesh.shape["head"])
    plan = block_plan if sizes == (16, 2) else general_plan
    return jax.shard_map(plan, mesh=mesh, in_specs=placed, out_specs=P("ctx", "head"), check_vma=False)
```

```python
import functools
import math

import jax
import jax.numpy as jnp
from jax import lax
from jax.experimental import pallas as pl
from jax.experimental.pallas import tpu as pltpu
from jax.sharding import PartitionSpec as P

HD = 64
ANCH_DEV = 256
LIVE_MAX = 192
PAD = 16
QROWS = 2 * LIVE_MAX
SENT = 256
TILE = 128

EPS = 1e-06
NEG = -1e30
MARK = 2.0**50
MARKED = 2.0**40
RATE = HD**-0.5 * math.log2(math.e)

ALL = ("ctx", "head")
F32 = jnp.float32
BF16 = jnp.bfloat16


def params(mib=32):
    return pltpu.CompilerParams(vmem_limit_bytes=mib * 2**20)


def vmem(count):
    return [pl.BlockSpec(memory_space=pltpu.VMEM)] * count


def dot(a, b, contract=((1,), (0,))):
    return lax.dot_general(a, b, (contract, ((), ())), preferred_element_type=F32)


COPIES = 4
GROUP = 8


def pool_kernel(sides, anchors_hbm, messages_hbm, *refs):
    outs = refs[: len(sides)]
    anchors_smem, listed, anchors, messages, sems = refs[len(sides) :]
    partitions = lax.axis_size("ctx")
    center = lax.axis_index("ctx")
    tiles = anchors.shape[0]
    rows = tiles // COPIES * TILE
    loads = [
        pltpu.make_async_copy(anchors_hbm, anchors_smem, sems.at[COPIES]),
        pltpu.make_async_copy(anchors_hbm, anchors, sems.at[COPIES + 1]),
    ]
    for part in range(COPIES):
        at = pl.ds(part * rows, rows)
        loads.append(pltpu.make_async_copy(messages_hbm.at[at], messages.at[at], sems.at[part]))
    for load in loads:
        load.start()
    for out in outs:
        out[...] = jnp.zeros_like(out)
    slots = lax.broadcasted_iota(jnp.int32, (LIVE_MAX, TILE), 0)
    loads[0].wait()
    half = tiles // 2
    for part in range(2):
        counts = [jnp.int32(0)] * len(sides)
        for tile in range(part * half, (part + 1) * half):
            side = lax.rem(anchors_smem[tile, 0] // ANCH_DEV - center + 1 + partitions, partitions)
            for index, name in enumerate(sides):
                ahead = 1 if name == "own" else 2 * lax.rem(center, 2)
                which = 2 - ahead if name == "near" else ahead
                listed[index, counts[index]] = tile
                counts[index] = counts[index] + jnp.where(side == which, 1, 0)
        if part == 0:
            loads[1].wait()
        for load in loads[2 + part * COPIES // 2 : 2 + (part + 1) * COPIES // 2]:
            load.wait()
        for index, out in enumerate(outs):

            def add(group, unused, index=index, out=out, count=counts[index]):
                onehots, parts = [], []
                for at in range(GROUP):
                    place = group * GROUP + at
                    wanted = place < count
                    tile = jnp.where(wanted, listed[index, jnp.minimum(place, half - 1)], 0)
                    slot = jnp.where(wanted, anchors[pl.ds(tile, 1), :] % ANCH_DEV, -1)
                    onehots.append(jnp.where(slots == slot, 1.0, 0.0).astype(BF16))
                    parts.append(messages[pl.ds(pl.multiple_of(tile * TILE, TILE), TILE), :])
                out[...] += dot(jnp.concatenate(onehots, axis=1), jnp.concatenate(parts, axis=0))
                return unused

            lax.fori_loop(0, (counts[index] + GROUP - 1) // GROUP, add, 0)


def pool(messages, node_anchor, sides):
    nodes, channels = messages.shape
    tiles = nodes // TILE
    hbm = pl.BlockSpec(memory_space=pltpu.MemorySpace.HBM)
    return pl.pallas_call(
        functools.partial(pool_kernel, sides),
        in_specs=[hbm] * 2,
        out_specs=vmem(len(sides)),
        scratch_shapes=[
            pltpu.SMEM((tiles, TILE), jnp.int32),
            pltpu.SMEM((len(sides), tiles + 1), jnp.int32),
            pltpu.VMEM((tiles, TILE), jnp.int32),
            pltpu.VMEM((nodes, channels), BF16),
            pltpu.SemaphoreType.DMA((COPIES + 2,)),
        ],
        out_shape=[jax.ShapeDtypeStruct((LIVE_MAX, channels), F32)] * len(sides),
        compiler_params=params(56),
        cost_estimate=pl.CostEstimate(flops=10**9, bytes_accessed=5 * 10**6, transcendentals=0),
        name="pool",
    )(node_anchor.reshape(tiles, TILE), messages)


def after_kernel(a_ref, *rest):
    rest[-1][...] = a_ref[...]


def after(a, *others, cost=1):
    return pl.pallas_call(
        after_kernel,
        in_specs=vmem(1) + [pl.BlockSpec(memory_space=pl.ANY)] * len(others),
        out_specs=pl.BlockSpec(memory_space=pltpu.VMEM),
        out_shape=jax.ShapeDtypeStruct(a.shape, a.dtype),
        compiler_params=params(),
        cost_estimate=pl.CostEstimate(flops=cost, bytes_accessed=1, transcendentals=0),
        name="after",
    )(a, *others)


def settle_kernel(count_ref, own_ref, far_ref, near_ref, out_ref):
    total = own_ref[...] + far_ref[...] + near_ref[...]
    slot = lax.broadcasted_iota(jnp.int32, total.shape, 0)
    out_ref[...] = jnp.where(slot < count_ref[0], total, MARK).astype(BF16)


def settle(count, own, far, near):
    return pl.pallas_call(
        settle_kernel,
        in_specs=[pl.BlockSpec(memory_space=pltpu.SMEM)] + vmem(3),
        out_specs=pl.BlockSpec(memory_space=pltpu.VMEM),
        out_shape=jax.ShapeDtypeStruct(own.shape, BF16),
        compiler_params=params(),
        name="settle",
    )(count, own, far, near)


def join_kernel(a_ref, b_ref, *rest):
    out_ref = rest[-1]
    rows = a_ref.shape[0]
    out_ref[:rows, :] = a_ref[...]
    out_ref[rows:, :] = b_ref[...]


def join(a, b, *others, cost=1):
    return pl.pallas_call(
        join_kernel,
        in_specs=vmem(2) + [pl.BlockSpec(memory_space=pl.ANY)] * len(others),
        out_specs=pl.BlockSpec(memory_space=pltpu.VMEM),
        out_shape=jax.ShapeDtypeStruct((a.shape[0] + b.shape[0], a.shape[1]), a.dtype),
        compiler_params=params(),
        cost_estimate=pl.CostEstimate(flops=cost, bytes_accessed=1, transcendentals=0),
        name="join",
    )(a, b, *others)


def normalise(mine, other, gain_ref, x):
    channels = mine.shape[1]
    mine, other = mine.astype(F32), other.astype(F32)
    dead = mine[:, :1] > MARKED
    square = jnp.sum(mine * mine + other * other, axis=1, keepdims=True)
    inverse = jnp.where(dead, 0.0, lax.rsqrt(square * (1.0 / (2 * channels)) + EPS))
    mine = (mine * inverse * gain_ref[x]).astype(BF16)
    other = (other * inverse * gain_ref[1 - x]).astype(BF16)
    return mine, other, dead


def project(mine, other, w_ref, x):
    return (dot(mine, w_ref[x]) + dot(other, w_ref[1 - x])).astype(BF16)


def query_kernel(first_ref, second_ref, gain_ref, wq_ref, query_ref, normed_ref):
    core = lax.rem(lax.axis_index("ctx"), 2)
    x = lax.axis_index("head")
    other = jnp.where(core == 0, second_ref[:LIVE_MAX, :], first_ref[LIVE_MAX:, :])
    mine, other, unused = normalise(first_ref[:LIVE_MAX, :], other, gain_ref, x)
    query_ref[...] = project(mine, other, wq_ref, x)
    normed_ref[...] = mine


def make_queries(first, second, gain, wq):
    channels = first.shape[1]
    return pl.pallas_call(
        query_kernel,
        in_specs=vmem(4),
        out_specs=vmem(2),
        out_shape=[jax.ShapeDtypeStruct((LIVE_MAX, channels), BF16)] * 2,
        compiler_params=params(),
        cost_estimate=pl.CostEstimate(flops=10**10, bytes_accessed=1, transcendentals=0),
        name="queries",
    )(first, second, gain, wq)


def attend_kernel(first_call, *refs):
    if first_call:
        qm, qr, first_ref, second_ref, gain_ref, wk_ref, wv_ref, out_ref = refs
        state_ref = None
    else:
        qm, qr, first_ref, second_ref, gain_ref, wk_ref, wv_ref, state_ref, out_ref = refs
    core = lax.rem(lax.axis_index("ctx"), 2)
    x = lax.axis_index("head")
    channels = first_ref.shape[1]
    heads = channels // HD
    one, two = first_ref[LIVE_MAX:, :], second_ref[:LIVE_MAX, :]
    mine = jnp.concatenate([first_ref[:LIVE_MAX, :], jnp.where(core == 0, one, two)], axis=0)
    other = jnp.concatenate([jnp.where(core == 0, two, one), second_ref[LIVE_MAX:, :]], axis=0)
    mine, other, dead = normalise(mine, other, gain_ref, x)
    keys = project(mine, other, wk_ref, x)
    values = project(mine, other, wv_ref, x)
    shut = jnp.where(dead, NEG, 0.0).astype(BF16)

    live = jnp.sum(jnp.where(dead, 0.0, 1.0), axis=0, keepdims=True)
    live = jnp.broadcast_to(live, (1, SENT))
    value_sum = jnp.sum(values.astype(F32), axis=0, keepdims=True)
    extra = channels + 2 * heads
    for part in range(channels // SENT):
        at = value_sum[:, part * SENT : (part + 1) * SENT]
        row = slice(extra + part, extra + part + 1)
        out_ref[row, QROWS - SENT :] = at if first_call else at + state_ref[row, QROWS - SENT :]
    row = slice(extra + channels // SENT, extra + channels // SENT + 1)
    out_ref[row, QROWS - SENT :] = live if first_call else live + state_ref[row, QROWS - SENT :]
    values = values.T

    lane_k = lax.broadcasted_iota(jnp.int32, (keys.shape[0], 128), 1)
    lane_q = lax.broadcasted_iota(jnp.int32, (QROWS, 128), 1)

    def score(head):
        pair, side = head // 2, head % 2
        at = slice(pair * 128, (pair + 1) * 128)
        query = jnp.concatenate([qm[:, at], qr[128:, at], qr[:128, at]], axis=0)
        hot = jnp.where(lane_q == (1 - side) * HD, 1.0, 0.0).astype(BF16)
        q = jnp.where((lane_q // HD) == side, query, hot)
        k = jnp.where((lane_k // HD) == side, keys[:, at], shut)
        return dot(k, q, ((1,), (1,)))

    def weigh(head, scores):
        top = jnp.max(scores, axis=0, keepdims=True)
        at_top = slice(channels + head, channels + head + 1)
        at_total = slice(channels + heads + head, channels + heads + head + 1)
        fade = None
        if not first_call:
            old_top = state_ref[at_top, :]
            top = jnp.maximum(top, old_top)
            fade = jnp.exp2((old_top - top) * RATE)
        weights = jnp.exp2((scores - top) * RATE)
        total = jnp.sum(weights, axis=0, keepdims=True)
        if not first_call:
            total = total + state_ref[at_total, :] * fade
        out_ref[at_top, :] = top
        out_ref[at_total, :] = total
        return weights.astype(BF16), fade

    def mix(head, weights, fade):
        at = slice(head * HD, (head + 1) * HD)
        mixed = dot(values[at], weights)
        if not first_call:
            mixed = mixed + state_ref[at, :] * fade
        out_ref[at, :] = mixed

    scores = [score(head) for head in range(heads // 2)]
    weights = []
    for head in range(heads):
        weights.append(weigh(head, scores[head]))
        if len(scores) < heads:
            scores.append(score(len(scores)))
    for head in range(heads):
        mix(head, *weights[head])


def attend(qm, qr, first, second, gain, wk, wv, state=None):
    channels = first.shape[1]
    args = [qm, qr, first, second, gain, wk, wv] + ([] if state is None else [state])
    keys = 2 * LIVE_MAX
    return pl.pallas_call(
        functools.partial(attend_kernel, state is None),
        in_specs=vmem(len(args)),
        out_specs=pl.BlockSpec(memory_space=pltpu.VMEM),
        out_shape=jax.ShapeDtypeStruct((channels + 2 * (channels // HD) + 8, QROWS), F32),
        input_output_aliases={} if state is None else {len(args) - 1: 0},
        compiler_params=params(),
        cost_estimate=pl.CostEstimate(
            flops=2*10**9, bytes_accessed=1, transcendentals=0
        ),
        name="attend",
    )(*args)


def combine_kernel(mine_ref, other_ref, out_ref):
    channels = out_ref.shape[1]
    heads = channels // HD

    def theirs(at):
        middle = other_ref[at, :128]
        return jnp.concatenate([other_ref[at, 128:], middle[:, 64:], middle[:, :64]], axis=1)

    for head in range(heads):
        at_top = slice(channels + head, channels + head + 1)
        at_total = slice(channels + heads + head, channels + heads + head + 1)
        at = slice(head * HD, (head + 1) * HD)
        a, b = mine_ref[at_top, :SENT], theirs(at_top)
        top = jnp.maximum(a, b)
        a, b = jnp.exp2((a - top) * RATE), jnp.exp2((b - top) * RATE)
        total = mine_ref[at_total, :SENT] * a + theirs(at_total) * b
        mixed = mine_ref[at, :SENT] * (a / total) + theirs(at) * (b / total)
        out_ref[:LIVE_MAX, at] = mixed.T[:LIVE_MAX].astype(BF16)
    extra = channels + 2 * heads
    sums = mine_ref[extra : extra + 8, QROWS - SENT :] + other_ref[extra : extra + 8, :]
    parts = channels // SENT
    live = sums[parts : parts + 1, :]
    for part in range(parts):
        mean = (sums[part : part + 1, :] / live).astype(BF16)
        out_ref[LIVE_MAX:, part * SENT : (part + 1) * SENT] = jnp.broadcast_to(mean, (PAD, SENT))


def combine(mine, other):
    channels = other.shape[0] // (HD + 2) * HD
    return pl.pallas_call(
        combine_kernel,
        in_specs=vmem(2),
        out_specs=pl.BlockSpec(memory_space=pltpu.VMEM),
        out_shape=jax.ShapeDtypeStruct((LIVE_MAX + PAD, channels), BF16),
        compiler_params=params(),
        name="combine",
    )(mine, other)


def own_branch_kernel(attended_ref, w_ref, out_ref):
    out_ref[...] = dot(attended_ref[...], w_ref[lax.axis_index("head")])


def own_branch(attended, w_out):
    return pl.pallas_call(
        own_branch_kernel,
        in_specs=vmem(2),
        out_specs=pl.BlockSpec(memory_space=pltpu.VMEM),
        out_shape=jax.ShapeDtypeStruct((attended.shape[0], w_out.shape[2]), F32),
        compiler_params=params(),
        cost_estimate=pl.CostEstimate(flops=10**8, bytes_accessed=10**6, transcendentals=0),
        name="own_branch",
    )(attended, w_out)


def finish_kernel(branch_ref, attended_ref, w_ref, normed_ref, out_ref):
    branch = branch_ref[...] + dot(attended_ref[...], w_ref[1 - lax.axis_index("head")])
    out_ref[:LIVE_MAX, :] = (branch[:LIVE_MAX] + normed_ref[...].astype(F32)).astype(BF16)
    rest = out_ref.shape[0] - LIVE_MAX
    out_ref[LIVE_MAX:, :] = jnp.broadcast_to(branch[LIVE_MAX : LIVE_MAX + 1], (rest, branch.shape[1])).astype(BF16)


def finish(branch, attended, w_out, normed):
    return pl.pallas_call(
        finish_kernel,
        in_specs=vmem(4),
        out_specs=pl.BlockSpec(memory_space=pltpu.VMEM),
        out_shape=jax.ShapeDtypeStruct((ANCH_DEV, branch.shape[1]), BF16),
        compiler_params=params(),
        name="finish",
    )(branch, attended, w_out, normed)


def pairs(move):
    found = []
    for z in range(4):
        for y in range(2):
            for core in range(2):
                for x in range(2):
                    to_z, to_y, to_core, to_x = move(z, y, core, x)
                    found.append((((z * 2 + y) * 2 + core) * 2 + x, ((to_z * 2 + to_y) * 2 + to_core) * 2 + to_x))
    return found


def send(array, move):
    return lax.ppermute(array, ALL, pairs(move))


def across_core(z, y, core, x):
    return z, y, 1 - core, x


def across_x(z, y, core, x):
    return z, y, core, 1 - x


def across_first(z, y, core, x):
    return (z, 1 - y, core, x) if core == 0 else (z, y, core, 1 - x)


def across_second(z, y, core, x):
    return (z, 1 - y, core, x) if core == 1 else (z, y, core, 1 - x)


def across_z(step):
    return lambda z, y, core, x: (z ^ step, y, core, x)


def halves(w):
    return w.reshape(2, w.shape[0] // 2, w.shape[1])


def block_plan(messages, node_anchor, anchor_count, norm_gain, w_query, w_key, w_value, w_out):
    channels = messages.shape[1]
    far, near = pool(messages, node_anchor, ("far", "near"))
    (own,) = pool(messages, node_anchor, ("own",))
    from_far = lax.ppermute(far, "ctx", [(i, (i + (1 if i % 2 else 15)) % 16) for i in range(16)])
    from_near = send(near, across_core)
    own = after(own, cost=10**9)
    mine = settle(anchor_count, own, from_far, from_near)
    gain = norm_gain.reshape(2, 1, channels)
    wq, wk, wv, wo = halves(w_query), halves(w_key), halves(w_value), halves(w_out)
    far_rows = [send(mine, across_z(step)) for step in (2, 3)]
    first = join(mine, send(mine, across_first))
    second = send(first, across_second)
    query, normed = make_queries(first, second, gain, wq)
    swapped = send(query, across_core)
    beside = [send(first, across_z(1)), send(second, across_z(1))]
    state = attend(query, swapped, first, second, gain, wk, wv)
    states = [state, attend(query, swapped, *beside, gain, wk, wv, state)]
    gates = (first, query)
    for index, rows in enumerate(far_rows):
        rows = after(rows, gates[index], cost=(2 * 10**10, 5 * 10**9)[index])
        first = join(rows, send(rows, across_first), *([] if index else [state]), cost=3 * 10**10)
        second = send(first, across_second)
        states.append(attend(query, swapped, first, second, gain, wk, wv, states[-1]))
    state = states[-1]
    other = send(state[:, QROWS - SENT :], across_core)
    attended = combine(state, other)
    attended_other = send(attended, across_x)
    branch = own_branch(attended, wo)
    return finish(branch, attended_other, wo, normed)


def shift(x, by):
    peers = lax.axis_size("ctx")
    return lax.ppermute(x, "ctx", [(i, (i + by) % peers) for i in range(peers)])


def pool_local(messages, node_anchor, center):
    partitions = lax.axis_size("ctx")
    owner_dev = node_anchor // ANCH_DEV
    offset = (owner_dev - center + 1 + partitions) % partitions
    local_slot = node_anchor % ANCH_DEV
    channel_count = messages.shape[1]
    tile_count = messages.shape[0] // 128
    group = math.gcd(tile_count, 4)
    steps_count = tile_count // group
    slot_blocks = local_slot.reshape(steps_count, group, 128)
    offset_blocks = offset.reshape(steps_count, group, 128)[:, :, 0]
    message_blocks = messages.reshape(steps_count, group, 128, channel_count)
    columns = jnp.arange(ANCH_DEV, dtype=jnp.int32)

    def add_block(running, pieces):
        slot_block, offset_block, message_block = pieces
        onehot = (slot_block[:, :, None] == columns[None, None, :]).astype(jnp.bfloat16)
        partial_value = jnp.einsum(
            "tnk,tnc->tkc", onehot, message_block, preferred_element_type=jnp.float32
        )
        for tile in range(group):
            where = offset_block[tile]
            current = lax.dynamic_index_in_dim(running, where, 0, keepdims=False)
            running = lax.dynamic_update_index_in_dim(
                running, current + partial_value[tile], where, 0
            )
        return (running, None)

    initial = jnp.zeros((3, ANCH_DEV, channel_count), jnp.float32)
    running, unused = lax.scan(add_block, initial, (slot_blocks, offset_blocks, message_blocks))
    return running


def make_fold(queries, shard_rows, scale):
    heads_local = queries.shape[1]

    def fold(carry, pieces, start_row):
        key_rows, value_rows, live_rows = pieces
        shards = live_rows.shape[0] // shard_rows
        key_blocks = key_rows.reshape(shards, shard_rows, heads_local, HD)
        value_blocks = value_rows.reshape(shards, shard_rows, heads_local, HD)
        live_blocks = live_rows.reshape(shards, shard_rows)

        def visit(state, block):
            highest, totals, accum = state
            key_block, value_block, live_block = block
            scores = (
                jnp.einsum("qhd,khd->hqk", queries, key_block, preferred_element_type=jnp.float32)
                * scale
            )
            alive = (live_block > 0)[None, None, :]
            scores = jnp.where(alive, scores, NEG)
            newest = jnp.maximum(highest, jnp.max(scores, axis=-1))
            weights = jnp.where(alive, jnp.exp(scores - newest[..., None]), 0.0)
            factor = jnp.exp(highest - newest)
            totals = totals * factor + jnp.sum(weights, axis=-1)
            mixed = jnp.einsum(
                "hqk,khd->hqd",
                weights.astype(jnp.bfloat16),
                value_block,
                preferred_element_type=jnp.float32,
            )
            accum = accum * factor[..., None] + mixed
            return ((newest, totals, accum), None)

        carry, unused = lax.scan(visit, carry, (key_blocks, value_blocks, live_blocks))
        return carry

    return fold


def general_plan(messages, node_anchor, anchor_count, norm_gain, w_query, w_key, w_value, w_out):
    center = lax.axis_index("ctx")
    pooled_terms = pool_local(messages, node_anchor, center)
    for_previous = pooled_terms[0]
    own_rows = pooled_terms[1]
    for_next = pooled_terms[2]
    from_next = shift(for_previous, -1)
    from_previous = shift(for_next, 1)
    sums = own_rows + from_next + from_previous
    pooled = sums.astype(jnp.bfloat16)
    whole = lax.all_gather(pooled, "head", axis=1, tiled=True).astype(jnp.float32)
    mean_square = jnp.mean(whole * whole, axis=1, keepdims=True)
    normed = (whole * lax.rsqrt(mean_square + EPS) * norm_gain).astype(jnp.bfloat16)
    channel_count = messages.shape[1]
    local_normed = lax.dynamic_slice_in_dim(
        normed, lax.axis_index("head") * channel_count, channel_count, 1
    )
    heads_local = w_query.shape[1] // HD
    queries = jnp.dot(normed, w_query, preferred_element_type=jnp.float32).astype(jnp.bfloat16)
    keys_local = jnp.dot(normed, w_key, preferred_element_type=jnp.float32).astype(jnp.bfloat16)
    values_local = jnp.dot(normed, w_value, preferred_element_type=jnp.float32).astype(jnp.bfloat16)
    queries = queries.reshape(ANCH_DEV, heads_local, HD)
    scale = HD ** (-0.5)
    initial = (
        jnp.full((heads_local, ANCH_DEV), NEG, jnp.float32),
        jnp.zeros((heads_local, ANCH_DEV), jnp.float32),
        jnp.zeros((heads_local, ANCH_DEV, HD), jnp.float32),
    )
    live_flags = (jnp.arange(ANCH_DEV, dtype=jnp.int32) < anchor_count[0]).astype(jnp.bfloat16)
    fold = make_fold(queries, ANCH_DEV, scale)
    highest, totals, accum = fold(
        initial,
        (
            lax.all_gather(keys_local, "ctx", axis=0, tiled=True),
            lax.all_gather(values_local, "ctx", axis=0, tiled=True),
            lax.all_gather(live_flags, "ctx", axis=0, tiled=True),
        ),
        jnp.int32(0),
    )
    attended = (
        (accum / totals[..., None])
        .transpose(1, 0, 2)
        .reshape(ANCH_DEV, heads_local * HD)
        .astype(jnp.bfloat16)
    )
    branch = jnp.dot(
        lax.all_gather(attended, "head", axis=1, tiled=True),
        w_out,
        preferred_element_type=jnp.float32,
    )
    return (local_normed.astype(jnp.float32) + branch).astype(jnp.bfloat16)


def solution(mesh):
    placed = (
        P("ctx", "head"),
        P("ctx"),
        P("ctx"),
        P(),
        P(None, "head"),
        P(None, "head"),
        P(None, "head"),
        P(None, "head"),
    )
    sizes = (mesh.shape["ctx"], mesh.shape["head"])
    plan = block_plan if sizes == (16, 2) else general_plan
    return jax.shard_map(plan, mesh=mesh, in_specs=placed, out_specs=P("ctx", "head"), check_vma=False)
```

```python
import functools
import math

import jax
import jax.numpy as jnp
from jax import lax
from jax.experimental import pallas as pl
from jax.experimental.pallas import tpu as pltpu
from jax.sharding import PartitionSpec as P

HD = 64
ANCH_DEV = 256
LIVE_MAX = 192
PAD = 16
QROWS = 2 * LIVE_MAX
SENT = 256
TILE = 128

EPS = 1e-06
NEG = -1e30
MARK = 2.0**50
MARKED = 2.0**40
RATE = HD**-0.5 * math.log2(math.e)

ALL = ("ctx", "head")
F32 = jnp.float32
BF16 = jnp.bfloat16


def params(mib=32):
    return pltpu.CompilerParams(vmem_limit_bytes=mib * 2**20)


def vmem(count):
    return [pl.BlockSpec(memory_space=pltpu.VMEM)] * count


def dot(a, b, contract=((1,), (0,))):
    return lax.dot_general(a, b, (contract, ((), ())), preferred_element_type=F32)


COPIES = 2
GROUP = 8


def pool_kernel(sides, anchors_hbm, messages_hbm, *refs):
    outs = refs[: len(sides)]
    anchors_smem, listed, anchors, messages, sems = refs[len(sides) :]
    partitions = lax.axis_size("ctx")
    center = lax.axis_index("ctx")
    tiles = anchors.shape[0]
    rows = tiles // COPIES * TILE
    loads = [
        pltpu.make_async_copy(anchors_hbm, anchors_smem, sems.at[COPIES]),
        pltpu.make_async_copy(anchors_hbm, anchors, sems.at[COPIES + 1]),
    ]
    for part in range(COPIES):
        at = pl.ds(part * rows, rows)
        loads.append(pltpu.make_async_copy(messages_hbm.at[at], messages.at[at], sems.at[part]))
    for load in loads:
        load.start()
    for out in outs:
        out[...] = jnp.zeros_like(out)
    slots = lax.broadcasted_iota(jnp.int32, (LIVE_MAX, TILE), 0)
    loads[0].wait()
    half = tiles // 2
    for part in range(2):
        counts = [jnp.int32(0)] * len(sides)
        for tile in range(part * half, (part + 1) * half):
            side = lax.rem(anchors_smem[tile, 0] // ANCH_DEV - center + 1 + partitions, partitions)
            for index, name in enumerate(sides):
                ahead = 1 if name == "own" else 2 * lax.rem(center, 2)
                which = 2 - ahead if name == "near" else ahead
                listed[index, counts[index]] = tile
                counts[index] = counts[index] + jnp.where(side == which, 1, 0)
        if part == 0:
            loads[1].wait()
        for load in loads[2 + part * COPIES // 2 : 2 + (part + 1) * COPIES // 2]:
            load.wait()
        for index, out in enumerate(outs):

            def add(group, unused, index=index, out=out, count=counts[index]):
                onehots, parts = [], []
                for at in range(GROUP):
                    place = group * GROUP + at
                    wanted = place < count
                    tile = jnp.where(wanted, listed[index, jnp.minimum(place, half - 1)], 0)
                    slot = jnp.where(wanted, anchors[pl.ds(tile, 1), :] % ANCH_DEV, -1)
                    onehots.append(jnp.where(slots == slot, 1.0, 0.0).astype(BF16))
                    parts.append(messages[pl.ds(pl.multiple_of(tile * TILE, TILE), TILE), :])
                out[...] += dot(jnp.concatenate(onehots, axis=1), jnp.concatenate(parts, axis=0))
                return unused

            lax.fori_loop(0, (counts[index] + GROUP - 1) // GROUP, add, 0)


def pool(messages, node_anchor, sides):
    nodes, channels = messages.shape
    tiles = nodes // TILE
    hbm = pl.BlockSpec(memory_space=pltpu.MemorySpace.HBM)
    return pl.pallas_call(
        functools.partial(pool_kernel, sides),
        in_specs=[hbm] * 2,
        out_specs=vmem(len(sides)),
        scratch_shapes=[
            pltpu.SMEM((tiles, TILE), jnp.int32),
            pltpu.SMEM((len(sides), tiles + 1), jnp.int32),
            pltpu.VMEM((tiles, TILE), jnp.int32),
            pltpu.VMEM((nodes, channels), BF16),
            pltpu.SemaphoreType.DMA((COPIES + 2,)),
        ],
        out_shape=[jax.ShapeDtypeStruct((LIVE_MAX, channels), F32)] * len(sides),
        compiler_params=params(56),
        cost_estimate=pl.CostEstimate(flops=10**9, bytes_accessed=5 * 10**6, transcendentals=0),
        name="pool",
    )(node_anchor.reshape(tiles, TILE), messages)


def after_kernel(a_ref, *rest):
    rest[-1][...] = a_ref[...]


def after(a, *others, cost=1):
    return pl.pallas_call(
        after_kernel,
        in_specs=vmem(1) + [pl.BlockSpec(memory_space=pl.ANY)] * len(others),
        out_specs=pl.BlockSpec(memory_space=pltpu.VMEM),
        out_shape=jax.ShapeDtypeStruct(a.shape, a.dtype),
        compiler_params=params(),
        cost_estimate=pl.CostEstimate(flops=cost, bytes_accessed=1, transcendentals=0),
        name="after",
    )(a, *others)


def settle_kernel(count_ref, own_ref, far_ref, near_ref, out_ref):
    total = own_ref[...] + far_ref[...] + near_ref[...]
    slot = lax.broadcasted_iota(jnp.int32, total.shape, 0)
    out_ref[...] = jnp.where(slot < count_ref[0], total, MARK).astype(BF16)


def settle(count, own, far, near):
    return pl.pallas_call(
        settle_kernel,
        in_specs=[pl.BlockSpec(memory_space=pltpu.SMEM)] + vmem(3),
        out_specs=pl.BlockSpec(memory_space=pltpu.VMEM),
        out_shape=jax.ShapeDtypeStruct(own.shape, BF16),
        compiler_params=params(),
        name="settle",
    )(count, own, far, near)


def join_kernel(a_ref, b_ref, *rest):
    out_ref = rest[-1]
    rows = a_ref.shape[0]
    out_ref[:rows, :] = a_ref[...]
    out_ref[rows:, :] = b_ref[...]


def join(a, b, *others, cost=1):
    return pl.pallas_call(
        join_kernel,
        in_specs=vmem(2) + [pl.BlockSpec(memory_space=pl.ANY)] * len(others),
        out_specs=pl.BlockSpec(memory_space=pltpu.VMEM),
        out_shape=jax.ShapeDtypeStruct((a.shape[0] + b.shape[0], a.shape[1]), a.dtype),
        compiler_params=params(),
        cost_estimate=pl.CostEstimate(flops=cost, bytes_accessed=1, transcendentals=0),
        name="join",
    )(a, b, *others)


def normalise(mine, other, gain_ref, x):
    channels = mine.shape[1]
    mine, other = mine.astype(F32), other.astype(F32)
    dead = mine[:, :1] > MARKED
    square = jnp.sum(mine * mine + other * other, axis=1, keepdims=True)
    inverse = jnp.where(dead, 0.0, lax.rsqrt(square * (1.0 / (2 * channels)) + EPS))
    mine = (mine * inverse * gain_ref[x]).astype(BF16)
    other = (other * inverse * gain_ref[1 - x]).astype(BF16)
    return mine, other, dead


def project(mine, other, w_ref, x):
    return (dot(mine, w_ref[x]) + dot(other, w_ref[1 - x])).astype(BF16)


def query_kernel(first_ref, second_ref, gain_ref, wq_ref, query_ref, normed_ref):
    core = lax.rem(lax.axis_index("ctx"), 2)
    x = lax.axis_index("head")
    other = jnp.where(core == 0, second_ref[:LIVE_MAX, :], first_ref[LIVE_MAX:, :])
    mine, other, unused = normalise(first_ref[:LIVE_MAX, :], other, gain_ref, x)
    query_ref[...] = project(mine, other, wq_ref, x)
    normed_ref[...] = mine


def make_queries(first, second, gain, wq):
    channels = first.shape[1]
    return pl.pallas_call(
        query_kernel,
        in_specs=vmem(4),
        out_specs=vmem(2),
        out_shape=[jax.ShapeDtypeStruct((LIVE_MAX, channels), BF16)] * 2,
        compiler_params=params(),
        cost_estimate=pl.CostEstimate(flops=10**10, bytes_accessed=1, transcendentals=0),
        name="queries",
    )(first, second, gain, wq)


def attend_kernel(first_call, *refs):
    if first_call:
        qm, qr, first_ref, second_ref, gain_ref, wk_ref, wv_ref, out_ref = refs
        state_ref = None
    else:
        qm, qr, first_ref, second_ref, gain_ref, wk_ref, wv_ref, state_ref, out_ref = refs
    core = lax.rem(lax.axis_index("ctx"), 2)
    x = lax.axis_index("head")
    channels = first_ref.shape[1]
    heads = channels // HD
    one, two = first_ref[LIVE_MAX:, :], second_ref[:LIVE_MAX, :]
    mine = jnp.concatenate([first_ref[:LIVE_MAX, :], jnp.where(core == 0, one, two)], axis=0)
    other = jnp.concatenate([jnp.where(core == 0, two, one), second_ref[LIVE_MAX:, :]], axis=0)
    mine, other, dead = normalise(mine, other, gain_ref, x)
    keys = project(mine, other, wk_ref, x)
    values = project(mine, other, wv_ref, x)
    shut = jnp.where(dead, NEG, 0.0).astype(BF16)

    live = jnp.sum(jnp.where(dead, 0.0, 1.0), axis=0, keepdims=True)
    live = jnp.broadcast_to(live, (1, SENT))
    value_sum = jnp.sum(values.astype(F32), axis=0, keepdims=True)
    extra = channels + 2 * heads
    for part in range(channels // SENT):
        at = value_sum[:, part * SENT : (part + 1) * SENT]
        row = slice(extra + part, extra + part + 1)
        out_ref[row, QROWS - SENT :] = at if first_call else at + state_ref[row, QROWS - SENT :]
    row = slice(extra + channels // SENT, extra + channels // SENT + 1)
    out_ref[row, QROWS - SENT :] = live if first_call else live + state_ref[row, QROWS - SENT :]
    values = values.T

    lane_k = lax.broadcasted_iota(jnp.int32, (keys.shape[0], 128), 1)
    lane_q = lax.broadcasted_iota(jnp.int32, (QROWS, 128), 1)

    def score(head):
        pair, side = head // 2, head % 2
        at = slice(pair * 128, (pair + 1) * 128)
        query = jnp.concatenate([qm[:, at], qr[128:, at], qr[:128, at]], axis=0)
        hot = jnp.where(lane_q == (1 - side) * HD, 1.0, 0.0).astype(BF16)
        q = jnp.where((lane_q // HD) == side, query, hot)
        k = jnp.where((lane_k // HD) == side, keys[:, at], shut)
        return dot(k, q, ((1,), (1,)))

    def weigh(head, scores):
        top = jnp.max(scores, axis=0, keepdims=True)
        at_top = slice(channels + head, channels + head + 1)
        at_total = slice(channels + heads + head, channels + heads + head + 1)
        fade = None
        if not first_call:
            old_top = state_ref[at_top, :]
            top = jnp.maximum(top, old_top)
            fade = jnp.exp2((old_top - top) * RATE)
        weights = jnp.exp2((scores - top) * RATE)
        total = jnp.sum(weights, axis=0, keepdims=True)
        if not first_call:
            total = total + state_ref[at_total, :] * fade
        out_ref[at_top, :] = top
        out_ref[at_total, :] = total
        return weights.astype(BF16), fade

    def mix(head, weights, fade):
        at = slice(head * HD, (head + 1) * HD)
        mixed = dot(values[at], weights)
        if not first_call:
            mixed = mixed + state_ref[at, :] * fade
        out_ref[at, :] = mixed

    scores = [score(head) for head in range(heads // 2)]
    weights = []
    for head in range(heads):
        weights.append(weigh(head, scores[head]))
        if len(scores) < heads:
            scores.append(score(len(scores)))
    for head in range(heads):
        mix(head, *weights[head])


def attend(qm, qr, first, second, gain, wk, wv, state=None):
    channels = first.shape[1]
    args = [qm, qr, first, second, gain, wk, wv] + ([] if state is None else [state])
    keys = 2 * LIVE_MAX
    return pl.pallas_call(
        functools.partial(attend_kernel, state is None),
        in_specs=vmem(len(args)),
        out_specs=pl.BlockSpec(memory_space=pltpu.VMEM),
        out_shape=jax.ShapeDtypeStruct((channels + 2 * (channels // HD) + 8, QROWS), F32),
        input_output_aliases={} if state is None else {len(args) - 1: 0},
        compiler_params=params(),
        cost_estimate=pl.CostEstimate(
            flops=2*10**9, bytes_accessed=1, transcendentals=0
        ),
        name="attend",
    )(*args)


def combine_kernel(mine_ref, other_ref, out_ref):
    channels = out_ref.shape[1]
    heads = channels // HD

    def theirs(at):
        middle = other_ref[at, :128]
        return jnp.concatenate([other_ref[at, 128:], middle[:, 64:], middle[:, :64]], axis=1)

    for head in range(heads):
        at_top = slice(channels + head, channels + head + 1)
        at_total = slice(channels + heads + head, channels + heads + head + 1)
        at = slice(head * HD, (head + 1) * HD)
        a, b = mine_ref[at_top, :SENT], theirs(at_top)
        top = jnp.maximum(a, b)
        a, b = jnp.exp2((a - top) * RATE), jnp.exp2((b - top) * RATE)
        total = mine_ref[at_total, :SENT] * a + theirs(at_total) * b
        mixed = mine_ref[at, :SENT] * (a / total) + theirs(at) * (b / total)
        out_ref[:LIVE_MAX, at] = mixed.T[:LIVE_MAX].astype(BF16)
    extra = channels + 2 * heads
    sums = mine_ref[extra : extra + 8, QROWS - SENT :] + other_ref[extra : extra + 8, :]
    parts = channels // SENT
    live = sums[parts : parts + 1, :]
    for part in range(parts):
        mean = (sums[part : part + 1, :] / live).astype(BF16)
        out_ref[LIVE_MAX:, part * SENT : (part + 1) * SENT] = jnp.broadcast_to(mean, (PAD, SENT))


def combine(mine, other):
    channels = other.shape[0] // (HD + 2) * HD
    return pl.pallas_call(
        combine_kernel,
        in_specs=vmem(2),
        out_specs=pl.BlockSpec(memory_space=pltpu.VMEM),
        out_shape=jax.ShapeDtypeStruct((LIVE_MAX + PAD, channels), BF16),
        compiler_params=params(),
        name="combine",
    )(mine, other)


def own_branch_kernel(attended_ref, w_ref, out_ref):
    out_ref[...] = dot(attended_ref[...], w_ref[lax.axis_index("head")])


def own_branch(attended, w_out):
    return pl.pallas_call(
        own_branch_kernel,
        in_specs=vmem(2),
        out_specs=pl.BlockSpec(memory_space=pltpu.VMEM),
        out_shape=jax.ShapeDtypeStruct((attended.shape[0], w_out.shape[2]), F32),
        compiler_params=params(),
        cost_estimate=pl.CostEstimate(flops=10**8, bytes_accessed=10**6, transcendentals=0),
        name="own_branch",
    )(attended, w_out)


def finish_kernel(branch_ref, attended_ref, w_ref, normed_ref, out_hbm, out, sems):
    w = w_ref.at[1 - lax.axis_index("head")]
    parts = sems.shape[0]
    width = out.shape[1] // parts
    rest = out.shape[0] - LIVE_MAX
    stores = []
    for part in range(parts):
        at = slice(part * width, (part + 1) * width)
        branch = branch_ref[:, at] + dot(attended_ref[...], w[:, at])
        out[:LIVE_MAX, at] = (branch[:LIVE_MAX] + normed_ref[:, at].astype(F32)).astype(BF16)
        out[LIVE_MAX:, at] = jnp.broadcast_to(branch[LIVE_MAX : LIVE_MAX + 1], (rest, width)).astype(BF16)
        stores.append(pltpu.make_async_copy(out.at[:, at], out_hbm.at[:, at], sems.at[part]))
        stores[-1].start()
    for store in stores:
        store.wait()


def finish(branch, attended, w_out, normed):
    shape = (ANCH_DEV, branch.shape[1])
    return pl.pallas_call(
        finish_kernel,
        in_specs=vmem(4),
        out_specs=pl.BlockSpec(memory_space=pl.ANY),
        out_shape=jax.ShapeDtypeStruct(shape, BF16),
        scratch_shapes=[pltpu.VMEM(shape, BF16), pltpu.SemaphoreType.DMA((2,))],
        compiler_params=params(),
        name="finish",
    )(branch, attended, w_out, normed)


def pairs(move):
    found = []
    for z in range(4):
        for y in range(2):
            for core in range(2):
                for x in range(2):
                    to_z, to_y, to_core, to_x = move(z, y, core, x)
                    found.append((((z * 2 + y) * 2 + core) * 2 + x, ((to_z * 2 + to_y) * 2 + to_core) * 2 + to_x))
    return found


def send(array, move):
    return lax.ppermute(array, ALL, pairs(move))


def across_core(z, y, core, x):
    return z, y, 1 - core, x


def across_x(z, y, core, x):
    return z, y, core, 1 - x


def across_first(z, y, core, x):
    return (z, 1 - y, core, x) if core == 0 else (z, y, core, 1 - x)


def across_second(z, y, core, x):
    return (z, 1 - y, core, x) if core == 1 else (z, y, core, 1 - x)


def across_z(step):
    return lambda z, y, core, x: (z ^ step, y, core, x)


def halves(w):
    return w.reshape(2, w.shape[0] // 2, w.shape[1])


def block_plan(messages, node_anchor, anchor_count, norm_gain, w_query, w_key, w_value, w_out):
    channels = messages.shape[1]
    far, near = pool(messages, node_anchor, ("far", "near"))
    (own,) = pool(messages, node_anchor, ("own",))
    from_far = lax.ppermute(far, "ctx", [(i, (i + (1 if i % 2 else 15)) % 16) for i in range(16)])
    from_near = send(near, across_core)
    own = after(own, cost=10**9)
    mine = settle(anchor_count, own, from_far, from_near)
    gain = norm_gain.reshape(2, 1, channels)
    wq, wk, wv, wo = halves(w_query), halves(w_key), halves(w_value), halves(w_out)
    far_rows = [send(mine, across_z(step)) for step in (2, 3)]
    first = join(mine, send(mine, across_first))
    second = send(first, across_second)
    query, normed = make_queries(first, second, gain, wq)
    swapped = send(query, across_core)
    beside = [send(first, across_z(1)), send(second, across_z(1))]
    state = attend(query, swapped, first, second, gain, wk, wv)
    states = [state, attend(query, swapped, *beside, gain, wk, wv, state)]
    gates = (first, query)
    for index, rows in enumerate(far_rows):
        rows = after(rows, gates[index], cost=(2 * 10**10, 5 * 10**9)[index])
        first = join(rows, send(rows, across_first), *([] if index else [state]), cost=3 * 10**10)
        second = send(first, across_second)
        states.append(attend(query, swapped, first, second, gain, wk, wv, states[-1]))
    state = states[-1]
    other = send(state[:, QROWS - SENT :], across_core)
    attended = combine(state, other)
    attended_other = send(attended, across_x)
    branch = own_branch(attended, wo)
    return finish(branch, attended_other, wo, normed)


def shift(x, by):
    peers = lax.axis_size("ctx")
    return lax.ppermute(x, "ctx", [(i, (i + by) % peers) for i in range(peers)])


def pool_local(messages, node_anchor, center):
    partitions = lax.axis_size("ctx")
    owner_dev = node_anchor // ANCH_DEV
    offset = (owner_dev - center + 1 + partitions) % partitions
    local_slot = node_anchor % ANCH_DEV
    channel_count = messages.shape[1]
    tile_count = messages.shape[0] // 128
    group = math.gcd(tile_count, 4)
    steps_count = tile_count // group
    slot_blocks = local_slot.reshape(steps_count, group, 128)
    offset_blocks = offset.reshape(steps_count, group, 128)[:, :, 0]
    message_blocks = messages.reshape(steps_count, group, 128, channel_count)
    columns = jnp.arange(ANCH_DEV, dtype=jnp.int32)

    def add_block(running, pieces):
        slot_block, offset_block, message_block = pieces
        onehot = (slot_block[:, :, None] == columns[None, None, :]).astype(jnp.bfloat16)
        partial_value = jnp.einsum(
            "tnk,tnc->tkc", onehot, message_block, preferred_element_type=jnp.float32
        )
        for tile in range(group):
            where = offset_block[tile]
            current = lax.dynamic_index_in_dim(running, where, 0, keepdims=False)
            running = lax.dynamic_update_index_in_dim(
                running, current + partial_value[tile], where, 0
            )
        return (running, None)

    initial = jnp.zeros((3, ANCH_DEV, channel_count), jnp.float32)
    running, unused = lax.scan(add_block, initial, (slot_blocks, offset_blocks, message_blocks))
    return running


def make_fold(queries, shard_rows, scale):
    heads_local = queries.shape[1]

    def fold(carry, pieces, start_row):
        key_rows, value_rows, live_rows = pieces
        shards = live_rows.shape[0] // shard_rows
        key_blocks = key_rows.reshape(shards, shard_rows, heads_local, HD)
        value_blocks = value_rows.reshape(shards, shard_rows, heads_local, HD)
        live_blocks = live_rows.reshape(shards, shard_rows)

        def visit(state, block):
            highest, totals, accum = state
            key_block, value_block, live_block = block
            scores = (
                jnp.einsum("qhd,khd->hqk", queries, key_block, preferred_element_type=jnp.float32)
                * scale
            )
            alive = (live_block > 0)[None, None, :]
            scores = jnp.where(alive, scores, NEG)
            newest = jnp.maximum(highest, jnp.max(scores, axis=-1))
            weights = jnp.where(alive, jnp.exp(scores - newest[..., None]), 0.0)
            factor = jnp.exp(highest - newest)
            totals = totals * factor + jnp.sum(weights, axis=-1)
            mixed = jnp.einsum(
                "hqk,khd->hqd",
                weights.astype(jnp.bfloat16),
                value_block,
                preferred_element_type=jnp.float32,
            )
            accum = accum * factor[..., None] + mixed
            return ((newest, totals, accum), None)

        carry, unused = lax.scan(visit, carry, (key_blocks, value_blocks, live_blocks))
        return carry

    return fold


def general_plan(messages, node_anchor, anchor_count, norm_gain, w_query, w_key, w_value, w_out):
    center = lax.axis_index("ctx")
    pooled_terms = pool_local(messages, node_anchor, center)
    for_previous = pooled_terms[0]
    own_rows = pooled_terms[1]
    for_next = pooled_terms[2]
    from_next = shift(for_previous, -1)
    from_previous = shift(for_next, 1)
    sums = own_rows + from_next + from_previous
    pooled = sums.astype(jnp.bfloat16)
    whole = lax.all_gather(pooled, "head", axis=1, tiled=True).astype(jnp.float32)
    mean_square = jnp.mean(whole * whole, axis=1, keepdims=True)
    normed = (whole * lax.rsqrt(mean_square + EPS) * norm_gain).astype(jnp.bfloat16)
    channel_count = messages.shape[1]
    local_normed = lax.dynamic_slice_in_dim(
        normed, lax.axis_index("head") * channel_count, channel_count, 1
    )
    heads_local = w_query.shape[1] // HD
    queries = jnp.dot(normed, w_query, preferred_element_type=jnp.float32).astype(jnp.bfloat16)
    keys_local = jnp.dot(normed, w_key, preferred_element_type=jnp.float32).astype(jnp.bfloat16)
    values_local = jnp.dot(normed, w_value, preferred_element_type=jnp.float32).astype(jnp.bfloat16)
    queries = queries.reshape(ANCH_DEV, heads_local, HD)
    scale = HD ** (-0.5)
    initial = (
        jnp.full((heads_local, ANCH_DEV), NEG, jnp.float32),
        jnp.zeros((heads_local, ANCH_DEV), jnp.float32),
        jnp.zeros((heads_local, ANCH_DEV, HD), jnp.float32),
    )
    live_flags = (jnp.arange(ANCH_DEV, dtype=jnp.int32) < anchor_count[0]).astype(jnp.bfloat16)
    fold = make_fold(queries, ANCH_DEV, scale)
    highest, totals, accum = fold(
        initial,
        (
            lax.all_gather(keys_local, "ctx", axis=0, tiled=True),
            lax.all_gather(values_local, "ctx", axis=0, tiled=True),
            lax.all_gather(live_flags, "ctx", axis=0, tiled=True),
        ),
        jnp.int32(0),
    )
    attended = (
        (accum / totals[..., None])
        .transpose(1, 0, 2)
        .reshape(ANCH_DEV, heads_local * HD)
        .astype(jnp.bfloat16)
    )
    branch = jnp.dot(
        lax.all_gather(attended, "head", axis=1, tiled=True),
        w_out,
        preferred_element_type=jnp.float32,
    )
    return (local_normed.astype(jnp.float32) + branch).astype(jnp.bfloat16)


def solution(mesh):
    placed = (
        P("ctx", "head"),
        P("ctx"),
        P("ctx"),
        P(),
        P(None, "head"),
        P(None, "head"),
        P(None, "head"),
        P(None, "head"),
    )
    sizes = (mesh.shape["ctx"], mesh.shape["head"])
    plan = block_plan if sizes == (16, 2) else general_plan
    return jax.shard_map(plan, mesh=mesh, in_specs=placed, out_specs=P("ctx", "head"), check_vma=False)
```
